256 devices in a mesh: section: 2 (over z_lo), img: 16 (over x, z_hi), ch: 8 (over y, core).
Axes of the slice: x: 4, y: 4, z: 8 (z_hi: 4, z_lo: 2; z = z_hi * 2 + z_lo), core: 2. Of those that a mesh axis runs over, the one named last changes fastest.
Arguments:
- pixels: bfloat16 [32, 64, 28, 640], P('img', 'ch'), may hold values from -6 to 6
- first_gain: float32 [640], replicated, may hold values from 0.25 to 1.75
- first_shift: float32 [640], replicated, may hold values from -3 to 3
- first_kernel: bfloat16 [3, 3, 640, 640], P(None, None, 'img'), may hold values from -0.078125 to 0.078125
- projection: bfloat16 [640, 2560], P('img'), may hold values from -0.25 to 0.25
- second_gain: float32 [2560], replicated, may hold values from 0.25 to 1.75
- second_shift: float32 [2560], replicated, may hold values from -3 to 3
- second_kernel: bfloat16 [3, 3, 2560, 2560], P(None, None, ('img', 'ch')), may hold values from -0.0390625 to 0.0390625
Outputs:
- section_outputs: bfloat16 [2, 32, 32, 14, 2560], P('section', 'img', 'ch')
The draws below stay inside these ranges and needn't reach their ends.
All inputs are finite; a program needn't handle non-finite values.
Results may differ from the reference program's by a relative error of at most 0.013.
Values may be sent and summed in bfloat16 or wider, within the bound.
A program may use at most 128 MiB of HBM per device.

```python
import jax
import jax.numpy as jnp
from jax import lax

C1 = 640
C2 = 2560
W = 28
H = 64
HO = 32
WO = 14
IMAGES = 32


def shard_levels(rng, extent, cuts, low, high):
    level = 1.0
    for dim, blocks in cuts:
        draws = jax.random.uniform(jax.random.fold_in(jax.random.fold_in(rng, 6), dim), (blocks,), jnp.float32, low / len(cuts), high / len(cuts))
        level = level * jnp.repeat(jnp.exp(draws), extent[dim] // blocks).reshape((-1,) + (1,) * (len(extent) - 1 - dim))
    return level


def centred(rng, shape, width, bound, cuts=(), dtype=jnp.bfloat16):
    drawn = width * jax.random.normal(rng, shape, jnp.float32)
    if cuts:
        drawn = drawn * shard_levels(rng, shape, cuts, -0.22, 0.18)
    return jnp.clip(drawn, -bound, bound).astype(dtype)


def setup_inputs(seed: int = 0) -> dict:
    splits = jax.random.split(jax.random.key(seed), 9)
    pixels = centred(splits[0], (IMAGES, H, W, C1), 1.0, 6.0, ((0, 16), (1, 8)))
    first_gain = jnp.clip(1.0 + 0.15 * jax.random.normal(splits[1], (C1,), jnp.float32), 0.25, 1.75)
    first_shift = centred(splits[2], (C1,), 0.5, 3.0, (), jnp.float32)
    first_kernel = centred(splits[3], (3, 3, C1, C1), (9 * C1) ** -0.5, 0.078125, ((2, 16),))
    projection = centred(splits[4], (C1, C2), C1 ** -0.5, 0.25, ((0, 16),))
    second_gain = jnp.clip(1.0 + 0.15 * jax.random.normal(splits[5], (C2,), jnp.float32), 0.25, 1.75)
    second_shift = centred(splits[6], (C2,), 0.5, 3.0, (), jnp.float32)
    second_kernel = centred(splits[7], (3, 3, C2, C2), (9 * C2) ** -0.5, 0.0390625, ((2, 128),))
    return {"pixels": pixels, "first_gain": first_gain, "first_shift": first_shift, "first_kernel": first_kernel, "projection": projection, "second_gain": second_gain, "second_shift": second_shift, "second_kernel": second_kernel}


LAYOUT = ("NHWC", "HWIO", "NHWC")


def convolve(inputs, kernel, padding):
    return lax.conv_general_dilated(inputs, kernel, (1, 1), padding, dimension_numbers=LAYOUT, preferred_element_type=jnp.float32)


def reduce_resolution(value_entries):
    count, height, breadth, depth = value_entries.shape
    blocks = value_entries.reshape(count, height // 2, 2, breadth // 2, 2, depth)
    return jnp.sum(blocks, axis=(2, 4)) * 0.25


def reference(pixels, first_gain, first_shift, first_kernel, projection, second_gain, second_shift, second_kernel):
    normalized_input = jax.nn.relu(pixels.astype(jnp.float32) * first_gain + first_shift).astype(jnp.bfloat16)
    blended_result = convolve(normalized_input, first_kernel, ((1, 1), (1, 1))) + pixels.astype(jnp.float32)
    averaged_pixels = reduce_resolution(blended_result).astype(jnp.bfloat16)
    flat = averaged_pixels.reshape(IMAGES * HO * WO, C1)
    projected = jnp.dot(flat, projection, preferred_element_type=jnp.float32).astype(jnp.bfloat16)
    projected = projected.reshape(IMAGES, HO, WO, C2)
    second_in = jax.nn.relu(projected.astype(jnp.float32) * second_gain + second_shift).astype(jnp.bfloat16)
    block = convolve(second_in, second_kernel, ((1, 1), (1, 1))) + projected.astype(jnp.float32)
    return jnp.stack([projected, block.astype(jnp.bfloat16)])
```

```python
import jax
import jax.numpy as jnp
from jax import lax
from jax.experimental import pallas as pl
from jax.experimental.pallas import tpu as pltpu
from jax.sharding import PartitionSpec as P

MESH = pl.DeviceIdType.MESH
F32 = jnp.float32
BF16 = jnp.bfloat16
D = 640
SLAB = 160


def lanes(i):
    return pl.ds(pl.multiple_of(i * D, 128), D)


def rows(i, n):
    return pl.ds(pl.multiple_of(i * n, 16), n)


def dot(a, b):
    return jnp.dot(a, b, preferred_element_type=F32)


def kernel(
    pix, g1, s1, k1, pr, g2, s2, k2,
    out,
    pxp, hal_t, hal_b, wp, wy, pland, wall, pn, k1x, nb, nsel, bq, acc1, part, prx, rtmp,
    pb, plin, pjb, abuf, acc2, cp, cin, fb,
    s_px, r_px, s_ht, r_ht, s_hb, r_hb, s_k1, r_k1, s_kx, r_kx, s_pr, r_pr, s_wy, r_wy,
    s_h1, r_h1, s_h2, r_h2, s_h3, r_h3, s_dd, r_dd, s_pa, r_pa, s_pl, r_pl,
    s_pj, r_pj, s_c, r_c, s_f, r_f,
):
    s = lax.axis_index("section")
    img = lax.axis_index("img")
    ch = lax.axis_index("ch")
    x, zh = lax.div(img, 4), lax.rem(img, 4)
    y, c = lax.div(ch, 2), lax.rem(ch, 2)
    other = 1 - c
    way = 2 * s - 1

    def dev(s_, x_, zh_, y_, c_):
        return (s_, lax.rem(x_ + 8, 4) * 4 + lax.rem(zh_ + 8, 4), lax.rem(y_ + 8, 4) * 2 + c_)

    def remote(src, dst, ss, rs, to):
        return pltpu.make_async_remote_copy(
            src_ref=src, dst_ref=dst, send_sem=ss, recv_sem=rs, device_id=to, device_id_type=MESH
        )

    partner = dev(s, x, zh, y, other)
    pair = dev(1 - s, x, zh, y, c)
    outward = dev(1 - s, x, zh + way, y, c)

    def arrived(dst, rs):
        remote(dst, dst, rs, rs, partner).wait_recv()

    barrier = pltpu.get_barrier_semaphore()
    met = []
    for dx in range(4):
        for dy in range(4):
            for dc in range(2):
                if dx or dy or dc:
                    met.append(dev(s, x + dx, zh, y + dy, c if dc == 0 else other))
    for dx in range(4):
        for dc in range(2):
            met.append(dev(1 - s, x + dx, zh, y, c if dc == 0 else other))
    met.append(outward)
    met.append(dev(1 - s, x, zh + 2, y, c))
    for to in met:
        pl.semaphore_signal(barrier, inc=1, device_id=to, device_id_type=MESH)
    pl.semaphore_wait(barrier, len(met))

    px_copy = remote(pix, pxp, s_px, r_px, partner)
    px_copy.start()
    down = [
        remote(pix.at[:, pl.ds(7, 1)], hal_t, s_ht.at[k], r_ht, dev(s, x, zh, y + 1, k))
        for k in range(2)
    ]
    up = [
        remote(pix.at[:, pl.ds(0, 1)], hal_b, s_hb.at[k], r_hb, dev(s, x, zh, y - 1, k))
        for k in range(2)
    ]
    sends_down = jnp.logical_and(c == 1, y < 3)
    sends_up = jnp.logical_and(c == 0, y > 0)

    @pl.when(sends_down)
    def _():
        for cpy in down:
            cpy.start()

    @pl.when(sends_up)
    def _():
        for cpy in up:
            cpy.start()

    zq_off = (1 - s) * 3 * c + s * (1 + c)
    zq = lax.rem(zh + zq_off, 4)
    k1_sends = jnp.logical_not(jnp.logical_and(s == 1, c == 0))
    k1_gets = jnp.logical_not(jnp.logical_and(s == 0, c == 0))
    k1_to = dev(1 - s, x, zh + s - (1 - s) * (1 + c), y, c)
    k1_copies = [
        remote(k1.at[pl.ds(3 * q, 3)], k1x.at[x, pl.ds(3 * q, 3)], s_k1.at[q], r_k1.at[q], k1_to)
        for q in range(3)
    ]

    @pl.when(k1_sends)
    def _():
        for cpy in k1_copies:
            cpy.start()

    @pl.when(jnp.logical_not(k1_gets))
    def _():
        k1x[x] = k1[...]

    pr_copies = []
    for dx in range(1, 4):
        to = lax.rem(x + dx, 4)
        cpy = remote(
            pr.at[:, lanes(to)], pland.at[x], s_pr.at[dx - 1], r_pr.at[dx - 1], dev(s, to, zh, y, c)
        )
        cpy.start()
        pr_copies.append(cpy)
    pland[x] = pr[:, lanes(x)]

    for half, first, count in ((0, 0, 5), (1, 5, 4)):
        for t in range(count):
            wp[half, pl.ds(20 * t, 20), :] = k2[first + t]
        wp[half, pl.ds(20 * count, 112 - 20 * count), :] = jnp.zeros((112 - 20 * count, 4 * D), BF16)
    wy_copies = []
    for dy in range(4):
        for dc in range(2):
            if dy == 0 and dc == 0:
                continue
            ty = lax.rem(y + dy, 4)
            tc = c if dc == 0 else other
            k = dy * 2 + dc
            cpy = remote(
                wp.at[tc, :, lanes(ty)], wy.at[ch], s_wy.at[k], r_wy.at[k], dev(s, x, zh, ty, tc)
            )
            cpy.start()
            wy_copies.append(cpy)
    wy[ch] = wp[c, :, lanes(y)]

    nsel[...] = jnp.zeros_like(nsel)
    for k in range(3):
        for e in range(2):
            abuf[k, e, pl.ds(0, 16), :] = jnp.zeros((16, D), BF16)
            abuf[k, e, pl.ds(528, 16), :] = jnp.zeros((16, D), BF16)

    def norm(cells):
        n = jnp.maximum(cells.astype(F32) * g1[...] + s1[...], 0.0)
        return jnp.concatenate([n, jnp.zeros((4, D), F32)], axis=0).astype(BF16)

    def norm_rows(ref, base):
        def step(i, carry):
            e, r = lax.div(i, 8), lax.rem(i, 8)
            nb[e, base + r] = norm(ref[e, r])
            return carry

        lax.fori_loop(0, 16, step, 0)

    norm_rows(pix, 1 + 8 * c)

    for i in range(4):
        both = pix[s, 2 * i].astype(F32) + pix[s, 2 * i + 1].astype(F32)
        both = jnp.concatenate([both, jnp.zeros((4, D), F32)], axis=0)
        for b in range(5):
            rtmp[i, b] = both[:, 128 * b : 128 * b + 128]

    kx_copies = []

    def k1_forward(q):
        @pl.when(k1_gets)
        def _():
            arrived(k1x.at[x, pl.ds(3 * q, 3)], r_k1.at[q])

        for dx in range(1, 4):
            block = k1x.at[x, pl.ds(3 * q, 3)]
            cpy = remote(
                block, block, s_kx.at[dx - 1, q], r_kx.at[dx - 1, q], dev(s, x + dx, zh, y, c)
            )
            cpy.start()
            kx_copies.append(cpy)

    for q in range(3):
        k1_forward(q)

    for dy in range(4):
        for dc in range(2):
            if dy or dc:
                sy = lax.rem(y - dy + 4, 4)
                sc = c if dc == 0 else other
                arrived(wy.at[sy * 2 + sc], r_wy.at[dy * 2 + dc])
    for dx in range(1, 4):
        arrived(pland.at[lax.rem(x - dx + 4, 4)], r_pr.at[dx - 1])

    def packed(t):
        return jnp.concatenate([wy[k, pl.ds(20 * t, 20), :] for k in range(8)], axis=0)

    def at(core, j, z_):
        return wall.at[5 * core + j, rows(z_, SLAB)]

    @pl.when(c == 0)
    def _():
        for j in range(5):
            wall[j, rows(zh, SLAB), :] = packed(j)

    @pl.when(c == 1)
    def _():
        wall[5, rows(zh, SLAB), :] = jnp.concatenate([pland[k] for k in range(4)], axis=0)
        for j in range(1, 5):
            wall[5 + j, rows(zh, SLAB), :] = packed(j - 1)

    z1 = lax.rem(zh + way + 4, 4)
    z2 = lax.rem(zh - way + 4, 4)
    z3 = lax.rem(zh + 2, 4)
    zs = (zh, z1, z2, z3)
    chain = []

    def share(q, j):
        cpy = remote(at(c, j, zs[q]), at(c, j, zs[q]), s_dd.at[q, j], r_dd.at[q, j], partner)
        cpy.start()
        chain.append(cpy)

    def pass_on(q, j, ss, rs, to):
        cpy = remote(at(c, j, zs[q]), at(c, j, zs[q]), ss.at[j], rs.at[j], to)
        cpy.start()
        chain.append(cpy)

    for j in range(5):
        pass_on(0, j, s_h1, r_h1, outward)
    for j in range(5):
        share(0, j)

    def hop1(j):
        arrived(at(c, j, z1), r_h1.at[j])
        pass_on(1, j, s_h2, r_h2, pair)
        share(1, j)

    def hop2(j):
        arrived(at(c, j, z2), r_h2.at[j])
        pass_on(2, j, s_h3, r_h3, outward)
        share(2, j)

    def hop3(j):
        arrived(at(c, j, z3), r_h3.at[j])
        share(3, j)

    arrived(pxp, r_px)
    norm_rows(pxp, 1 + 8 * other)

    @pl.when(y > 0)
    def _():
        arrived(hal_t, r_ht)
        for e in range(2):
            nb[e, 0] = norm(hal_t[e, 0])

    @pl.when(y == 0)
    def _():
        nb[:, 0] = jnp.zeros((2, 32, D), BF16)

    @pl.when(y < 3)
    def _():
        arrived(hal_b, r_hb)
        for e in range(2):
            nb[e, 17] = norm(hal_b[e, 0])

    @pl.when(y == 3)
    def _():
        nb[:, 17] = jnp.zeros((2, 32, D), BF16)

    col = lax.broadcasted_iota(jnp.int32, (D, 256), 1)
    row = lax.broadcasted_iota(jnp.int32, (D, 256), 0)
    want = jnp.where(col < 160, col + lax.div(col, 40) * 120 + zq * 40, -1)
    select = jnp.where(row == want, 1.0, 0.0).astype(BF16)

    def select_rows(i, carry):
        e, b = lax.div(i, 3), lax.rem(i, 3)
        got = dot(nb[e, pl.ds(6 * b, 6)].reshape(192, D), select)
        for r in range(6):
            for h in range(2):
                nsel[h, e, 6 * b + r, pl.ds(8, 32), :] = got[32 * r : 32 * r + 32, 128 * h : 128 * h + 128]
        return carry

    lax.fori_loop(0, 6, select_rows, 0)

    def box(i, carry):
        e, r = lax.div(i, 9), lax.rem(i, 9)
        for par in range(2):
            for h in range(2):
                v = [
                    nsel[h, e, 2 * r + par, pl.ds(7 + d, 16, stride=2), :]
                    + nsel[h, e, 2 * r + par + 1, pl.ds(7 + d, 16, stride=2), :]
                    for d in range(4)
                ]
                for dx in range(3):
                    both = ((v[dx] + v[dx + 1]) * 0.25).astype(BF16)
                    bq[dx, par, e, r, :, pl.ds(128 * h, 128)] = both
        return carry

    lax.fori_loop(0, 18, box, 0)

    hop1(0)
    hop1(1)

    for dx in range(1, 4):
        for q in range(3):
            arrived(k1x.at[lax.rem(x - dx + 4, 4), pl.ds(3 * q, 3)], r_kx.at[dx - 1, q])
    for t in range(9):
        dy, dx = t // 3, t % 3
        w = jnp.concatenate([k1x[k, t] for k in range(4)], axis=0)
        a = bq[dx, dy % 2, :, pl.ds(dy // 2, 8), :, :].reshape(256, 256)[:, :160]
        got = dot(a, w)
        if t == 0:
            acc1[...] = got
        else:
            acc1[...] += got
    part[...] = acc1[...].astype(BF16)
    pa_copies = []
    for k in range(1, 4):
        ts = s if k < 2 else 1 - s
        tc = c if k % 2 == 0 else other
        cpy = remote(
            part.at[rows(ts * 2 + tc, 64)], prx.at[k - 1], s_pa.at[k - 1], r_pa.at[k - 1],
            dev(ts, x, zh, y, tc),
        )
        cpy.start()
        pa_copies.append(cpy)
    hop1(2)
    for k in range(3):
        arrived(prx.at[k], r_pa.at[k])
    total = acc1[rows(s * 2 + c, 64), :]
    for k in range(3):
        total += prx[k].astype(F32)
    rest = jnp.concatenate(
        [
            jnp.concatenate(
                [
                    rtmp[i, b, pl.ds(0, 16, stride=2), :] + rtmp[i, b, pl.ds(1, 16, stride=2), :]
                    for b in range(5)
                ],
                axis=1,
            )
            for i in range(4)
        ],
        axis=0,
    )
    pb[...] = (total + rest * 0.25).astype(BF16)

    core = lax.div(x, 2)
    slot = lax.rem(x, 2)
    pl_copies = []
    for dx in range(4):
        for dy in range(4):
            k = dx * 4 + dy
            cpy = remote(
                pb, plin.at[slot, rows(ch, 64)], s_pl.at[k], r_pl.at[slot * 8 + ch],
                dev(s, x + dx, zh, y + dy, core),
            )
            pl_copies.append(cpy)
            if k:
                cpy.start()

    @pl.when(core != c)
    def _():
        pl_copies[0].start()

    @pl.when(core == c)
    def _():
        plin[slot, rows(ch, 64), :] = pb[...]

    for j in range(3, 5):
        hop1(j)
    for j in range(5):
        hop2(j)
    hop3(0)

    for e in range(2):
        for k in range(8):
            own = jnp.logical_and(2 * c + e == x, ch == k)

            @pl.when(jnp.logical_not(own))
            def _(e=e, k=k):
                arrived(plin.at[e, pl.ds(64 * k, 64)], r_pl.at[e * 8 + k])

    @pl.when(c == 0)
    def _():
        for q in range(4):
            arrived(at(1, 0, zs[q]), r_dd.at[q, 0])

    pn[...] = jnp.concatenate(
        [wall[5, pl.ds(zb * SLAB + xb * 40, 40), :] for xb in range(4) for zb in range(4)], axis=0
    )
    gain, shift = g2[:, lanes(x)], s2[:, lanes(x)]
    inside = lax.rem(lax.broadcasted_iota(jnp.int32, (128, 1), 0), 16) < 14

    def project(i, carry):
        e, m = lax.div(i, 4), lax.rem(i, 4)
        p = dot(plin[e, rows(m, 128), :], pn[...]).astype(BF16)
        pjb[e, rows(m, 128), :] = p
        v = jnp.maximum(p.astype(F32) * gain + shift, 0.0)
        v = jnp.where(inside, v, 0.0)
        place = pl.ds(pl.multiple_of(128 * m + 16, 16), 128)
        abuf[0, e, place, :] = pltpu.roll(v, 1, 0).astype(BF16)
        abuf[1, e, place, :] = v.astype(BF16)
        abuf[2, e, place, :] = pltpu.roll(v, 127, 0).astype(BF16)
        return carry

    lax.fori_loop(0, 8, project, 0)

    pj_copies = []
    for e in range(2):
        for tc in range(2):
            own = jnp.logical_and(jnp.logical_and(s == 0, 2 * c + e == x), tc == c)
            src = pjb.at[e, rows(2 * y + tc, 64)]
            cpy = remote(
                src, out.at[s, :, lanes(x)], s_pj.at[2 * e + tc], r_pj.at[4 * s + x],
                dev(0, 2 * c + e, zh, y, tc),
            )
            pj_copies.append((own, cpy))

            @pl.when(jnp.logical_not(own))
            def _(cpy=cpy):
                cpy.start()

            @pl.when(own)
            def _(src=src):
                out[0, :, lanes(x)] = src[...]

    for j in range(1, 5):
        hop3(j)
    for q in range(4):
        for j in range(5):
            if j == 0:

                @pl.when(c == 1)
                def _(q=q):
                    arrived(at(0, 0, zs[q]), r_dd.at[q, 0])

            else:
                arrived(at(other, j, zs[q]), r_dd.at[q, j])

    adds = x == y

    def c_copy(e, k):
        return remote(
            cp.at[e, rows(k, 64)], cin.at[x * 4 + y], s_c.at[e * 8 + k], r_c.at[x * 4 + y],
            dev(s, 2 * c + e, zh, lax.div(k, 2), lax.rem(k, 2)),
        )

    def c_own(e, k):
        return jnp.logical_and(2 * c + e == x, k == ch)

    def second(i, carry):
        e, m = lax.div(i, 2), lax.rem(i, 2)
        for t in range(9):
            dy, dx = t // 3, t % 3
            a = abuf[dx, e, pl.ds(pl.multiple_of(256 * m + 16 * dy, 16), 256), :]
            got = dot(a, wall[t if t < 5 else t + 1])
            if t == 0:
                acc2[...] = got
            else:
                acc2[...] += got
        proj = pjb[e, rows(m, 256), :].astype(F32)
        cp[e, rows(m, 256), :] = (acc2[...] + jnp.where(adds, proj, 0.0)).astype(BF16)
        for q in range(4):
            k = 4 * m + q
            own = c_own(e, k)

            @pl.when(jnp.logical_not(own))
            def _(k=k):
                c_copy(e, k).start()

            @pl.when(own)
            def _(k=k):
                cin[x * 4 + y] = cp[e, rows(k, 64), :]

        return carry

    lax.fori_loop(0, 4, second, 0)

    f_copies = []
    for yb in range(4):
        total = jnp.zeros((64, D), F32)
        for xb in range(4):
            own = jnp.logical_and(jnp.logical_and(core == c, xb == x), yb == y)

            @pl.when(jnp.logical_not(own))
            def _(xb=xb, yb=yb):
                arrived(cin.at[xb * 4 + yb], r_c.at[xb * 4 + yb])

            total += cin[xb * 4 + yb].astype(F32)
        columns = pl.ds(yb * D, D)
        fb[:, columns] = total.astype(BF16)
        cpy = remote(fb.at[:, columns], out.at[0, :, columns], s_f.at[yb], r_f.at[yb], pair)
        f_copies.append(cpy)

        @pl.when(s == 0)
        def _(cpy=cpy):
            cpy.start()

        @pl.when(s == 1)
        def _(columns=columns):
            out[1, :, columns] = fb[:, columns]

    @pl.when(s == 0)
    def _():
        for sb in range(2):
            for xb in range(4):
                own = jnp.logical_and(jnp.logical_and(sb == 0, xb == x), core == c)

                @pl.when(jnp.logical_not(own))
                def _(sb=sb, xb=xb):
                    arrived(out.at[sb, :, pl.ds(xb * D, D)], r_pj.at[4 * sb + xb])

        for cpy in f_copies:
            cpy.wait_send()

    @pl.when(s == 1)
    def _():
        for yb in range(4):
            arrived(out.at[0, :, pl.ds(yb * D, D)], r_f.at[yb])

    for own, cpy in pj_copies:

        @pl.when(jnp.logical_not(own))
        def _(cpy=cpy):
            cpy.wait_send()

    for e in range(2):
        for k in range(8):

            @pl.when(jnp.logical_not(c_own(e, k)))
            def _(e=e, k=k):
                c_copy(e, k).wait_send()

    px_copy.wait_send()

    @pl.when(sends_down)
    def _():
        for cpy in down:
            cpy.wait_send()

    @pl.when(sends_up)
    def _():
        for cpy in up:
            cpy.wait_send()

    @pl.when(k1_sends)
    def _():
        for cpy in k1_copies:
            cpy.wait_send()

    @pl.when(core != c)
    def _():
        pl_copies[0].wait_send()

    for cpy in pr_copies + wy_copies + kx_copies + chain + pa_copies + pl_copies[1:]:
        cpy.wait_send()


def body(
    pixels,
    first_gain,
    first_shift,
    first_kernel,
    projection,
    second_gain,
    second_shift,
    second_kernel,
):
    dma = pltpu.SemaphoreType.DMA

    def vmem(*shape, dtype=BF16):
        return pltpu.VMEM(shape, dtype)

    counts = [
        (), (), (2,), (), (2,), (), (3,), (3,), (3, 3), (3, 3), (3,), (3,), (8,), (8,),
        (5,), (5,), (5,), (5,), (5,), (5,), (4, 5), (4, 5), (3,), (3,), (16,), (16,),
        (4,), (8,), (16,), (16,), (4,), (4,),
    ]
    result = pl.pallas_call(
        kernel,
        name="window",
        out_shape=jax.ShapeDtypeStruct((2, 64, 4 * D), BF16),
        in_specs=[pl.BlockSpec(memory_space=pltpu.VMEM)] * 8,
        out_specs=pl.BlockSpec(memory_space=pltpu.VMEM),
        scratch_shapes=[
            vmem(2, 8, 28, D),
            vmem(2, 1, 28, D),
            vmem(2, 1, 28, D),
            vmem(2, 112, 4 * D),
            vmem(8, 112, D),
            vmem(4, 40, D),
            vmem(10, D, D),
            vmem(D, D),
            vmem(4, 9, 40, D),
            vmem(2, 18, 32, D),
            vmem(2, 2, 19, 48, 128, dtype=F32),
            vmem(3, 2, 2, 9, 16, 256),
            vmem(256, D, dtype=F32),
            vmem(256, D),
            vmem(3, 64, D),
            vmem(4, 5, 32, 128, dtype=F32),
            vmem(64, D),
            vmem(2, 512, D),
            vmem(2, 512, D),
            vmem(3, 2, 544, D),
            vmem(256, D, dtype=F32),
            vmem(2, 512, D),
            vmem(16, 64, D),
            vmem(64, 4 * D),
        ]
        + [dma(n) for n in counts],
        compiler_params=pltpu.CompilerParams(
            collective_id=0, has_side_effects=True, vmem_limit_bytes=56 * 2**20
        ),
        cost_estimate=pl.CostEstimate(flops=8 * 10**9, bytes_accessed=10**7, transcendentals=0),
    )(
        pixels,
        first_gain[None],
        first_shift[None],
        first_kernel.reshape(9, 40, D),
        projection,
        second_gain[None],
        second_shift[None],
        second_kernel.reshape(9, 20, 4 * D),
    )
    return result.reshape(2, 4, 16, 4 * D)[None, :, :, :14]


def solution(mesh):
    placed = (
        P("img", "ch", None, None),
        P(),
        P(),
        P(None, None, "img", None),
        P("img", None),
        P(),
        P(),
        P(None, None, ("img", "ch"), None),
    )
    return jax.shard_map(
        body,
        mesh=mesh,
        in_specs=placed,
        out_specs=P("section", "img", "ch", None, None),
        check_vma=False,
    )
```

```python
import jax
import jax.numpy as jnp
from jax import lax
from jax.experimental import pallas as pl
from jax.experimental.pallas import tpu as pltpu
from jax.sharding import PartitionSpec as P

MESH = pl.DeviceIdType.MESH
F32 = jnp.float32
BF16 = jnp.bfloat16
D = 640
SLAB = 160


def lanes(i):
    return pl.ds(pl.multiple_of(i * D, 128), D)


def rows(i, n):
    return pl.ds(pl.multiple_of(i * n, 16), n)


def dot(a, b):
    return jnp.dot(a, b, preferred_element_type=F32)


def kernel(
    pix, g1, s1, k1, pr, g2, s2, k2,
    out,
    pxp, hal_t, hal_b, wp, wy, pland, wall, pn, k1x, nb, nsel, bq, acc1, part, prx, rtmp,
    pb, plin, pjb, abuf, acc2, cp, cin, fb, g2w, s2w,
    s_px, r_px, s_ht, r_ht, s_hb, r_hb, s_k1, r_k1, s_kx, r_kx, s_pr, r_pr, s_wy, r_wy,
    s_h1, r_h1, s_h2, r_h2, s_h3, r_h3, s_h4, r_h4, s_dd, r_dd, s_pa, r_pa, s_pl, r_pl,
    s_pj, r_pj, s_c, r_c, s_f, r_f,
):
    s = lax.axis_index("section")
    img = lax.axis_index("img")
    ch = lax.axis_index("ch")
    x, zh = lax.div(img, 4), lax.rem(img, 4)
    y, c = lax.div(ch, 2), lax.rem(ch, 2)
    other = 1 - c
    way = 2 * s - 1

    def dev(s_, x_, zh_, y_, c_):
        return (s_, lax.rem(x_ + 8, 4) * 4 + lax.rem(zh_ + 8, 4), lax.rem(y_ + 8, 4) * 2 + c_)

    def remote(src, dst, ss, rs, to):
        return pltpu.make_async_remote_copy(
            src_ref=src, dst_ref=dst, send_sem=ss, recv_sem=rs, device_id=to, device_id_type=MESH
        )

    partner = dev(s, x, zh, y, other)
    pair = dev(1 - s, x, zh, y, c)
    outward = dev(1 - s, x, zh + way, y, c)

    def arrived(dst, rs):
        remote(dst, dst, rs, rs, partner).wait_recv()

    barrier = pltpu.get_barrier_semaphore()
    met = []
    for dx in range(4):
        for dy in range(4):
            for dc in range(2):
                if dx or dy or dc:
                    met.append(dev(s, x + dx, zh, y + dy, c if dc == 0 else other))
    for dx in range(4):
        for dc in range(2):
            met.append(dev(1 - s, x + dx, zh, y, c if dc == 0 else other))
    met.append(outward)
    met.append(dev(1 - s, x, zh + 2, y, c))
    for to in met:
        pl.semaphore_signal(barrier, inc=1, device_id=to, device_id_type=MESH)
    diagonal = jnp.logical_and(c == 1, x == y)

    @pl.when(jnp.logical_and(c == 1, x != y))
    def _():
        to = dev(1 - s, y, zh - (1 - s) + 2 * s, y, c)
        pl.semaphore_signal(barrier, inc=1, device_id=to, device_id_type=MESH)

    pl.semaphore_wait(barrier, len(met) + jnp.where(diagonal, 3, 0))

    px_copy = remote(pix, pxp, s_px, r_px, partner)
    px_copy.start()
    down = [
        remote(pix.at[:, pl.ds(7, 1)], hal_t, s_ht.at[k], r_ht, dev(s, x, zh, y + 1, k))
        for k in range(2)
    ]
    up = [
        remote(pix.at[:, pl.ds(0, 1)], hal_b, s_hb.at[k], r_hb, dev(s, x, zh, y - 1, k))
        for k in range(2)
    ]
    sends_down = jnp.logical_and(c == 1, y < 3)
    sends_up = jnp.logical_and(c == 0, y > 0)

    @pl.when(sends_down)
    def _():
        for cpy in down:
            cpy.start()

    @pl.when(sends_up)
    def _():
        for cpy in up:
            cpy.start()

    zq_off = (1 - s) * 3 * c + s * (1 + c)
    zq = lax.rem(zh + zq_off, 4)
    line = jnp.where(c == 0, x, y)
    k1_gets = jnp.logical_not(jnp.logical_and(s == 0, c == 0))
    k1_sends = jnp.logical_and(c == 0, s == 0)
    k1_copies = [
        [
            remote(
                k1.at[pl.ds(3 * q, 3)], k1x.at[line, pl.ds(3 * q, 3)], s_k1.at[dx, q], r_k1.at[q],
                dev(1 - s, x + dx, zh + s - (1 - s) * (1 + c), y, c),
            )
            for q in range(3)
        ]
        for dx in range(4)
    ]

    @pl.when(k1_sends)
    def _():
        for cpy in k1_copies[0]:
            cpy.start()

    @pl.when(diagonal)
    def _():
        for q in range(3):
            for dx in (2, 1, 3, 0):
                k1_copies[dx][q].start()

    @pl.when(jnp.logical_not(k1_gets))
    def _():
        k1x[x] = k1[...]

    pr_copies = []
    for dx in range(1, 4):
        to = lax.rem(x + dx, 4)
        cpy = remote(
            pr.at[:, lanes(to)], pland.at[x], s_pr.at[dx - 1], r_pr.at[dx - 1], dev(s, to, zh, y, c)
        )
        cpy.start()
        pr_copies.append(cpy)
    pland[x] = pr[:, lanes(x)]

    wy_copies = []
    for part_at, size, taps in ((0, 48, (0, 1)), (48, 64, (2, 3, 4))):
        for half, first, count in ((0, 0, 5), (1, 5, 4)):
            used = 0
            for a in taps:
                if a < count:
                    wp[half, pl.ds(part_at + used, 20), :] = k2[first + a]
                    used += 20
            blank = size - used
            wp[half, pl.ds(part_at + used, blank), :] = jnp.zeros((blank, 4 * D), BF16)
        for dy in (2, 1, 3, 0):
            for dc in range(2):
                if dy == 0 and dc == 0:
                    continue
                ty = lax.rem(y + dy, 4)
                tc = c if dc == 0 else other
                k = (part_at // 48) * 8 + dy * 2 + dc
                cpy = remote(
                    wp.at[tc, pl.ds(part_at, size), lanes(ty)], wy.at[ch, pl.ds(part_at, size)],
                    s_wy.at[k], r_wy.at[k], dev(s, x, zh, ty, tc),
                )
                cpy.start()
                wy_copies.append(cpy)
    wy[ch] = wp[c, :, lanes(y)]

    g2w[...] = g2[...].reshape(1, 4 * D)
    s2w[...] = s2[...].reshape(1, 4 * D)
    gain1, shift1 = g1[...].reshape(1, D), s1[...].reshape(1, D)
    nsel[...] = jnp.zeros_like(nsel)
    for k in range(3):
        for e in range(2):
            abuf[k, e, pl.ds(0, 16), :] = jnp.zeros((16, D), BF16)
            abuf[k, e, pl.ds(528, 16), :] = jnp.zeros((16, D), BF16)

    def norm(cells):
        n = jnp.maximum(cells.astype(F32) * gain1 + shift1, 0.0)
        return jnp.concatenate([n, jnp.zeros((4, D), F32)], axis=0).astype(BF16)

    def norm_rows(ref, base):
        def step(i, carry):
            e, r = lax.div(i, 8), lax.rem(i, 8)
            nb[e, base + r] = norm(ref[e, r])
            return carry

        lax.fori_loop(0, 16, step, 0)

    norm_rows(pix, 1 + 8 * c)

    for i in range(4):
        both = pix[s, 2 * i].astype(F32) + pix[s, 2 * i + 1].astype(F32)
        both = jnp.concatenate([both, jnp.zeros((4, D), F32)], axis=0)
        for b in range(5):
            rtmp[i, b] = both[:, 128 * b : 128 * b + 128]

    kx_copies = []

    def k1_forward(q):
        block = k1x.at[line, pl.ds(3 * q, 3)]

        @pl.when(k1_gets)
        def _():
            arrived(block, r_k1.at[q])

        for d in (2, 1, 3):
            cpy = remote(
                block, block, s_kx.at[d - 1, q], r_kx.at[d - 1, q],
                dev(s, x + d * (1 - c), zh, y + d * c, c),
            )
            cpy.start()
            kx_copies.append(cpy)

    def wy_wait(part_at, size):
        for dy in range(4):
            for dc in range(2):
                if dy or dc:
                    sy = lax.rem(y - dy + 4, 4)
                    sc = c if dc == 0 else other
                    k = (part_at // 48) * 8 + dy * 2 + dc
                    arrived(wy.at[sy * 2 + sc, pl.ds(part_at, size)], r_wy.at[k])

    def packed(a):
        at_row = 20 * a if a < 2 else 48 + 20 * (a - 2)
        return jnp.concatenate([wy[k, pl.ds(at_row, 20), :] for k in range(8)], axis=0)

    def at(core, j, z_):
        return wall.at[5 * core + j, rows(z_, SLAB)]

    z1 = lax.rem(zh + way + 4, 4)
    z2 = lax.rem(zh - way + 4, 4)
    z3 = lax.rem(zh + 2, 4)
    zs = (zh, z1, z2, z3)
    chain = []
    shares = []
    side = lax.rem(s + c, 2)

    def share(q, j, n):
        k = len(shares)
        shares.append((q, j, n))
        block = wall.at[pl.ds(5 * c + j, n), rows(zs[q], SLAB)]
        cpy = remote(block, block, s_dd.at[k], r_dd.at[k], partner)
        cpy.start()
        chain.append(cpy)

    def link(q, j, ss, rs, to):
        return remote(at(c, j, zs[q]), at(c, j, zs[q]), ss.at[j], rs.at[j], to)

    def hop1(j):
        arrived(at(c, j, z1), r_h1.at[j])
        cpy = link(1, j, s_h2, r_h2, pair)
        cpy.start()
        chain.append(cpy)

    third = []
    fourth = []

    def hop2(j):
        arrived(at(c, j, z2), r_h2.at[j])
        cpy = link(2, j, s_h3, r_h3, outward)
        goes = side == (1 if j < 3 else 0)
        third.append((goes, cpy))

        @pl.when(goes)
        def _():
            cpy.start()

    def hop3(j):
        cpy = link(3, j, s_h4, r_h4, pair)
        comes = side == (0 if j < 3 else 1)
        fourth.append((comes, cpy))

        @pl.when(comes)
        def _():
            arrived(at(c, j, z3), r_h3.at[j])
            cpy.start()

        @pl.when(jnp.logical_not(comes))
        def _():
            arrived(at(c, j, z3), r_h4.at[j])

    def own_slabs(first, count):
        @pl.when(c == 0)
        def _():
            for j in range(first, first + count):
                wall[j, rows(zh, SLAB), :] = packed(j)

        @pl.when(c == 1)
        def _():
            for j in range(first, first + count):
                if j == 0:
                    w = jnp.concatenate([pland[k] for k in range(4)], axis=0)
                else:
                    w = packed(j - 1)
                wall[5 + j, rows(zh, SLAB), :] = w

        for j in range(first, first + count):
            cpy = link(0, j, s_h1, r_h1, outward)
            cpy.start()
            chain.append(cpy)
        share(0, first, count)

    k1_forward(0)
    wy_wait(0, 48)
    for dx in range(1, 4):
        arrived(pland.at[lax.rem(x - dx + 4, 4)], r_pr.at[dx - 1])
    own_slabs(0, 2)
    k1_forward(1)

    arrived(pxp, r_px)
    norm_rows(pxp, 1 + 8 * other)

    @pl.when(y > 0)
    def _():
        arrived(hal_t, r_ht)
        for e in range(2):
            nb[e, 0] = norm(hal_t[e, 0])

    @pl.when(y == 0)
    def _():
        nb[:, 0] = jnp.zeros((2, 32, D), BF16)

    @pl.when(y < 3)
    def _():
        arrived(hal_b, r_hb)
        for e in range(2):
            nb[e, 17] = norm(hal_b[e, 0])

    @pl.when(y == 3)
    def _():
        nb[:, 17] = jnp.zeros((2, 32, D), BF16)

    wy_wait(48, 64)
    own_slabs(2, 3)
    k1_forward(2)

    col = lax.broadcasted_iota(jnp.int32, (D, 256), 1)
    row = lax.broadcasted_iota(jnp.int32, (D, 256), 0)
    want = jnp.where(col < 160, col + lax.div(col, 40) * 120 + zq * 40, -1)
    select = jnp.where(row == want, 1.0, 0.0).astype(BF16)

    def select_rows(i, carry):
        e, b = lax.div(i, 3), lax.rem(i, 3)
        got = dot(nb[e, pl.ds(6 * b, 6)].reshape(192, D), select)
        for r in range(6):
            for h in range(2):
                nsel[h, e, 6 * b + r, pl.ds(8, 32), :] = got[32 * r : 32 * r + 32, 128 * h : 128 * h + 128]
        return carry

    lax.fori_loop(0, 6, select_rows, 0)

    def box(i, carry):
        e, r = lax.div(i, 9), lax.rem(i, 9)
        for par in range(2):
            for h in range(2):
                v = [
                    nsel[h, e, 2 * r + par, pl.ds(7 + d, 16, stride=2), :]
                    + nsel[h, e, 2 * r + par + 1, pl.ds(7 + d, 16, stride=2), :]
                    for d in range(4)
                ]
                for dx in range(3):
                    both = ((v[dx] + v[dx + 1]) * 0.25).astype(BF16)
                    bq[dx, par, e, r, :, pl.ds(128 * h, 128)] = both
        return carry

    lax.fori_loop(0, 18, box, 0)

    hop1(0)
    hop1(1)

    for q in range(3):
        for d in range(1, 4):
            arrived(k1x.at[lax.rem(line - d + 4, 4), pl.ds(3 * q, 3)], r_kx.at[d - 1, q])
        for t in range(3 * q, 3 * q + 3):
            dy, dx = t // 3, t % 3
            w = jnp.concatenate([k1x[k, t] for k in range(4)], axis=0)
            a = bq[dx, dy % 2, :, pl.ds(dy // 2, 8), :, :].reshape(256, 256)[:, :160]
            got = dot(a, w)
            if t == 0:
                acc1[...] = got
            else:
                acc1[...] += got
    part[...] = acc1[...].astype(BF16)
    pa_copies = []
    for k in range(1, 4):
        ts = s if k < 2 else 1 - s
        tc = c if k % 2 == 0 else other
        cpy = remote(
            part.at[rows(ts * 2 + tc, 64)], prx.at[k - 1], s_pa.at[k - 1], r_pa.at[k - 1],
            dev(ts, x, zh, y, tc),
        )
        cpy.start()
        pa_copies.append(cpy)
    hop1(2)
    for k in range(3):
        arrived(prx.at[k], r_pa.at[k])
    total = acc1[rows(s * 2 + c, 64), :]
    for k in range(3):
        total += prx[k].astype(F32)
    rest = jnp.concatenate(
        [
            jnp.concatenate(
                [
                    rtmp[i, b, pl.ds(0, 16, stride=2), :] + rtmp[i, b, pl.ds(1, 16, stride=2), :]
                    for b in range(5)
                ],
                axis=1,
            )
            for i in range(4)
        ],
        axis=0,
    )
    pb[...] = (total + rest * 0.25).astype(BF16)

    core = lax.div(x, 2)
    slot = lax.rem(x, 2)
    pl_copies = []
    for dx in (2, 1, 3, 0):
        for dy in (2, 1, 3, 0):
            k = dx * 4 + dy
            cpy = remote(
                pb, plin.at[slot, rows(ch, 64)], s_pl.at[k], r_pl.at[slot * 8 + ch],
                dev(s, x + dx, zh, y + dy, core),
            )
            pl_copies.append(cpy)
            if k:
                cpy.start()

    @pl.when(core != c)
    def _():
        pl_copies[-1].start()

    @pl.when(core == c)
    def _():
        plin[slot, rows(ch, 64), :] = pb[...]

    for j in range(3, 5):
        hop1(j)
    share(1, 0, 5)
    for j in range(5):
        hop2(j)
    share(2, 0, 5)
    hop3(0)
    share(3, 0, 1)

    def shared(k):
        q, j, n = shares[k]
        arrived(wall.at[pl.ds(5 * other + j, n), rows(zs[q], SLAB)], r_dd.at[k])

    for k in (0, 2, 3, 4):
        shared(k)

    pn[...] = jnp.concatenate(
        [wall[5, pl.ds(zb * SLAB + xb * 40, 40), :] for xb in range(4) for zb in range(4)], axis=0
    )
    gain, shift = g2w[:, lanes(x)], s2w[:, lanes(x)]
    inside = lax.rem(lax.broadcasted_iota(jnp.int32, (128, 1), 0), 16) < 14

    def nearest(i):
        return lax.rem(y + i + jnp.where(i == 2, 1, 0) - jnp.where(i == 3, 1, 0), 4)

    def project(i, carry):
        e, m = lax.rem(i, 2), nearest(lax.div(i, 2))
        for k in range(2):
            own = jnp.logical_and(2 * c + e == x, ch == 2 * m + k)

            @pl.when(jnp.logical_not(own))
            def _(k=k):
                arrived(plin.at[e, rows(2 * m + k, 64)], r_pl.at[e * 8 + 2 * m + k])

        p = dot(plin[e, rows(m, 128), :], pn[...]).astype(BF16)
        pjb[e, rows(m, 128), :] = p
        v = jnp.maximum(p.astype(F32) * gain + shift, 0.0)
        v = jnp.where(inside, v, 0.0)
        place = pl.ds(pl.multiple_of(128 * m + 16, 16), 128)
        abuf[0, e, place, :] = pltpu.roll(v, 1, 0).astype(BF16)
        abuf[1, e, place, :] = v.astype(BF16)
        abuf[2, e, place, :] = pltpu.roll(v, 127, 0).astype(BF16)
        return carry

    lax.fori_loop(0, 8, project, 0)

    pj_copies = []
    for e in range(2):
        for tc in range(2):
            own = jnp.logical_and(jnp.logical_and(s == 0, 2 * c + e == x), tc == c)
            src = pjb.at[e, rows(2 * y + tc, 64)]
            cpy = remote(
                src, out.at[s, :, lanes(x)], s_pj.at[2 * e + tc], r_pj.at[4 * s + x],
                dev(0, 2 * c + e, zh, y, tc),
            )
            pj_copies.append((own, cpy))

            @pl.when(jnp.logical_not(own))
            def _(cpy=cpy):
                cpy.start()

            @pl.when(own)
            def _(src=src):
                out[0, :, lanes(x)] = src[...]

    for j in range(1, 5):
        hop3(j)
    share(3, 1, 4)
    for k in (1, 5):
        shared(k)

    adds = x == y

    def c_copy(e, k):
        return remote(
            cp.at[e, rows(k, 64)], cin.at[x * 4 + y], s_c.at[e * 8 + k], r_c.at[x * 4 + y],
            dev(s, 2 * c + e, zh, lax.div(k, 2), lax.rem(k, 2)),
        )

    def c_own(e, k):
        return jnp.logical_and(2 * c + e == x, k == ch)

    def second(i, carry):
        e, m = lax.div(i, 2), lax.rem(i, 2)
        for t in range(9):
            dy, dx = t // 3, t % 3
            a = abuf[dx, e, pl.ds(pl.multiple_of(256 * m + 16 * dy, 16), 256), :]
            got = dot(a, wall[t if t < 5 else t + 1])
            if t == 0:
                acc2[...] = got
            else:
                acc2[...] += got
        proj = pjb[e, rows(m, 256), :].astype(F32)
        cp[e, rows(m, 256), :] = (acc2[...] + jnp.where(adds, proj, 0.0)).astype(BF16)
        for q in range(4):
            k = 4 * m + q
            own = c_own(e, k)

            @pl.when(jnp.logical_not(own))
            def _(k=k):
                c_copy(e, k).start()

            @pl.when(own)
            def _(k=k):
                cin[x * 4 + y] = cp[e, rows(k, 64), :]

        return carry

    lax.fori_loop(0, 4, second, 0)

    def finish(i, carry):
        yb = nearest(i)
        total = jnp.zeros((64, D), F32)
        for xb in range(4):
            own = jnp.logical_and(jnp.logical_and(core == c, xb == x), yb == y)

            @pl.when(jnp.logical_not(own))
            def _(xb=xb):
                arrived(cin.at[xb * 4 + yb], r_c.at[xb * 4 + yb])

            total += cin[xb * 4 + yb].astype(F32)
        fb[:, lanes(yb)] = total.astype(BF16)

        @pl.when(s == 0)
        def _():
            f_copy(yb).start()

        @pl.when(s == 1)
        def _():
            out[1, :, lanes(yb)] = fb[:, lanes(yb)]

        return carry

    def f_copy(yb):
        block = fb.at[:, lanes(yb)]
        return remote(block, out.at[0, :, lanes(yb)], s_f.at[yb], r_f.at[yb], pair)

    lax.fori_loop(0, 4, finish, 0)

    @pl.when(s == 0)
    def _():
        for sb in range(2):
            for xb in range(4):
                own = jnp.logical_and(jnp.logical_and(sb == 0, xb == x), core == c)

                @pl.when(jnp.logical_not(own))
                def _(sb=sb, xb=xb):
                    arrived(out.at[sb, :, pl.ds(xb * D, D)], r_pj.at[4 * sb + xb])

        for yb in range(4):
            f_copy(yb).wait_send()

    @pl.when(s == 1)
    def _():
        for yb in range(4):
            arrived(out.at[0, :, pl.ds(yb * D, D)], r_f.at[yb])

    for own, cpy in pj_copies:

        @pl.when(jnp.logical_not(own))
        def _(cpy=cpy):
            cpy.wait_send()

    for e in range(2):
        for k in range(8):

            @pl.when(jnp.logical_not(c_own(e, k)))
            def _(e=e, k=k):
                c_copy(e, k).wait_send()

    px_copy.wait_send()

    @pl.when(sends_down)
    def _():
        for cpy in down:
            cpy.wait_send()

    @pl.when(sends_up)
    def _():
        for cpy in up:
            cpy.wait_send()

    @pl.when(k1_sends)
    def _():
        for cpy in k1_copies[0]:
            cpy.wait_send()

    @pl.when(diagonal)
    def _():
        for line_copies in k1_copies:
            for cpy in line_copies:
                cpy.wait_send()

    for goes, cpy in third + fourth:

        @pl.when(goes)
        def _(cpy=cpy):
            cpy.wait_send()

    @pl.when(core != c)
    def _():
        pl_copies[-1].wait_send()

    for cpy in pr_copies + wy_copies + kx_copies + chain + pa_copies + pl_copies[:-1]:
        cpy.wait_send()


def body(
    pixels,
    first_gain,
    first_shift,
    first_kernel,
    projection,
    second_gain,
    second_shift,
    second_kernel,
):
    dma = pltpu.SemaphoreType.DMA

    def vmem(*shape, dtype=BF16):
        return pltpu.VMEM(shape, dtype)

    counts = [
        (), (), (2,), (), (2,), (), (4, 3), (3,), (3, 3), (3, 3), (3,), (3,), (16,), (16,),
        (5,), (5,), (5,), (5,), (5,), (5,), (5,), (5,), (6,), (6,), (3,), (3,), (16,), (16,),
        (4,), (8,), (16,), (16,), (4,), (4,),
    ]
    result = pl.pallas_call(
        kernel,
        name="window",
        out_shape=jax.ShapeDtypeStruct((2, 64, 4 * D), BF16),
        in_specs=[pl.BlockSpec(memory_space=pltpu.VMEM)] * 8,
        out_specs=pl.BlockSpec(memory_space=pltpu.VMEM),
        scratch_shapes=[
            vmem(2, 8, 28, D),
            vmem(2, 1, 28, D),
            vmem(2, 1, 28, D),
            vmem(2, 112, 4 * D),
            vmem(8, 112, D),
            vmem(4, 40, D),
            vmem(10, D, D),
            vmem(D, D),
            vmem(4, 9, 40, D),
            vmem(2, 18, 32, D),
            vmem(2, 2, 19, 48, 128, dtype=F32),
            vmem(3, 2, 2, 9, 16, 256),
            vmem(256, D, dtype=F32),
            vmem(256, D),
            vmem(3, 64, D),
            vmem(4, 5, 32, 128, dtype=F32),
            vmem(64, D),
            vmem(2, 512, D),
            vmem(2, 512, D),
            vmem(3, 2, 544, D),
            vmem(256, D, dtype=F32),
            vmem(2, 512, D),
            vmem(16, 64, D),
            vmem(64, 4 * D),
            vmem(1, 4 * D, dtype=F32),
            vmem(1, 4 * D, dtype=F32),
        ]
        + [dma(n) for n in counts],
        compiler_params=pltpu.CompilerParams(
            collective_id=0, has_side_effects=True, vmem_limit_bytes=56 * 2**20
        ),
        cost_estimate=pl.CostEstimate(flops=8 * 10**9, bytes_accessed=10**7, transcendentals=0),
    )(
        pixels,
        first_gain,
        first_shift,
        first_kernel.reshape(9, 40, D),
        projection,
        second_gain,
        second_shift,
        second_kernel.reshape(9, 20, 4 * D),
    )
    return result.reshape(2, 4, 16, 4 * D)[None, :, :, :14]


def solution(mesh):
    placed = (
        P("img", "ch", None, None),
        P(),
        P(),
        P(None, None, "img", None),
        P("img", None),
        P(),
        P(),
        P(None, None, ("img", "ch"), None),
    )
    return jax.shard_map(
        body,
        mesh=mesh,
        in_specs=placed,
        out_specs=P("section", "img", "ch", None, None),
        check_vma=False,
    )
```

```python
import jax
import jax.numpy as jnp
from jax import lax
from jax.experimental import pallas as pl
from jax.experimental.pallas import tpu as pltpu
from jax.sharding import PartitionSpec as P

MESH = pl.DeviceIdType.MESH
F32 = jnp.float32
BF16 = jnp.bfloat16
D = 640
SLAB = 160


PARTS = ((pl.ds(0, 48), pl.ds(0, 48)), (pl.ds(48, 32), pl.ds(48, 64)))


def lanes(i):
    return pl.ds(pl.multiple_of(i * D, 128), D)


def rows(i, n):
    return pl.ds(pl.multiple_of(i * n, 16), n)


def dot(a, b):
    return jnp.dot(a, b, preferred_element_type=F32)


def kernel(
    pix, g1, s1, k1, pr, g2, s2, k2,
    out,
    pxp, hal_t, hal_b, wp, wy, pland, wall, pn, k1x, nb, nsel, bq, acc1, part, prx, rtmp,
    pb, plin, pjb, abuf, cp, cin, fb, g2w, s2w,
    s_px, r_px, s_ht, r_ht, s_hb, r_hb, s_k1, r_k1, s_kx, r_kx, s_pr, r_pr, s_wy, r_wy,
    s_h1, r_h1, s_h2, r_h2, s_h3, r_h3, s_h4, r_h4, s_dd, r_dd, s_pa, r_pa, s_pl, r_pl,
    s_pj, r_pj, s_c, r_c, s_f, r_f,
):
    s = lax.axis_index("section")
    img = lax.axis_index("img")
    ch = lax.axis_index("ch")
    x, zh = lax.div(img, 4), lax.rem(img, 4)
    y, c = lax.div(ch, 2), lax.rem(ch, 2)
    other = 1 - c
    way = 2 * s - 1

    def dev(s_, x_, zh_, y_, c_):
        return (s_, lax.rem(x_ + 8, 4) * 4 + lax.rem(zh_ + 8, 4), lax.rem(y_ + 8, 4) * 2 + c_)

    def remote(src, dst, ss, rs, to):
        return pltpu.make_async_remote_copy(
            src_ref=src, dst_ref=dst, send_sem=ss, recv_sem=rs, device_id=to, device_id_type=MESH
        )

    partner = dev(s, x, zh, y, other)
    pair = dev(1 - s, x, zh, y, c)
    outward = dev(1 - s, x, zh + way, y, c)

    def arrived(dst, rs):
        remote(dst, dst, rs, rs, partner).wait_recv()

    barrier = pltpu.get_barrier_semaphore()
    met = []
    for dx in range(4):
        for dy in range(4):
            for dc in range(2):
                if dx or dy or dc:
                    met.append(dev(s, x + dx, zh, y + dy, c if dc == 0 else other))
    for dx in range(4):
        for dc in range(2):
            met.append(dev(1 - s, x + dx, zh, y, c if dc == 0 else other))
    met.append(outward)
    met.append(dev(1 - s, x, zh + 2, y, c))
    for to in met:
        pl.semaphore_signal(barrier, inc=1, device_id=to, device_id_type=MESH)
    pl.semaphore_wait(barrier, len(met))

    px_copy = remote(pix, pxp, s_px, r_px, partner)
    px_copy.start()
    down = [
        remote(pix.at[:, pl.ds(7, 1)], hal_t, s_ht.at[k], r_ht, dev(s, x, zh, y + 1, k))
        for k in range(2)
    ]
    up = [
        remote(pix.at[:, pl.ds(0, 1)], hal_b, s_hb.at[k], r_hb, dev(s, x, zh, y - 1, k))
        for k in range(2)
    ]
    sends_down = jnp.logical_and(c == 1, y < 3)
    sends_up = jnp.logical_and(c == 0, y > 0)

    @pl.when(sends_down)
    def _():
        for cpy in down:
            cpy.start()

    @pl.when(sends_up)
    def _():
        for cpy in up:
            cpy.start()

    zq_off = (1 - s) * 3 * c + s * (1 + c)
    zq = lax.rem(zh + zq_off, 4)
    line = jnp.where(c == 0, x, y)
    diagonal = jnp.logical_and(c == 1, x == y)
    k1_gets = jnp.logical_not(jnp.logical_and(s == 0, c == 0))
    k1_sends = jnp.logical_or(jnp.logical_and(c == 0, s == 0), diagonal)
    k1_copies = [
        remote(
            k1.at[pl.ds(3 * q, 3)], k1x.at[line, pl.ds(3 * q, 3)], s_k1.at[0, q], r_k1.at[q],
            dev(1 - s, x, zh + s - (1 - s) * (1 + c), y, c),
        )
        for q in range(3)
    ]

    @pl.when(k1_sends)
    def _():
        for cpy in k1_copies:
            cpy.start()

    @pl.when(jnp.logical_not(k1_gets))
    def _():
        k1x[x] = k1[...]

    pr_copies = []
    for dx in range(1, 4):
        to = lax.rem(x + dx, 4)
        cpy = remote(
            pr.at[:, lanes(to)], pland.at[x], s_pr.at[dx - 1], r_pr.at[dx - 1], dev(s, to, zh, y, c)
        )
        cpy.start()
        pr_copies.append(cpy)
    pland[x] = pr[:, lanes(x)]

    wy_copies = []
    for lower in range(2):
        for half, first, count in ((0, 0, 4), (1, 4, 5)):
            for a in range(3 * lower, 3 + 2 * lower):
                if a < count:
                    wp[half, pl.ds(20 * a, 20), :] = k2[first + a]
            if half and lower:
                wp[1, pl.ds(100, 12), :] = jnp.zeros((12, 4 * D), BF16)
        for dy in (2, 1, 3, 0):
            for dc in range(2):
                if dy == 0 and dc == 0:
                    continue
                ty = lax.rem(y + dy, 4)
                tc = c if dc == 0 else other
                k = lower * 8 + dy * 2 + dc
                for core in range(2):
                    part_rows = PARTS[lower][core]
                    cpy = remote(
                        wp.at[core, part_rows, lanes(ty)], wy.at[ch, part_rows],
                        s_wy.at[k], r_wy.at[k], dev(s, x, zh, ty, core),
                    )
                    wy_copies.append((tc == core, cpy))

                    @pl.when(tc == core)
                    def _(cpy=cpy):
                        cpy.start()

    wy[ch, pl.ds(0, 80), :] = wp[c, pl.ds(0, 80), lanes(y)]
    wy[ch, pl.ds(80, 32), :] = wp[1, pl.ds(80, 32), lanes(y)]

    g2w[...] = g2[...].reshape(1, 4 * D)
    s2w[...] = s2[...].reshape(1, 4 * D)
    gain1, shift1 = g1[...].reshape(1, D), s1[...].reshape(1, D)
    nsel[...] = jnp.zeros_like(nsel)
    for k in range(3):
        for e in range(2):
            abuf[k, e, pl.ds(0, 16), :] = jnp.zeros((16, D), BF16)
            abuf[k, e, pl.ds(528, 16), :] = jnp.zeros((16, D), BF16)

    def norm(cells):
        n = jnp.maximum(cells.astype(F32) * gain1 + shift1, 0.0)
        return jnp.concatenate([n, jnp.zeros((4, D), F32)], axis=0).astype(BF16)

    def norm_rows(ref, base):
        def step(i, carry):
            e, r = lax.div(i, 8), lax.rem(i, 8)
            nb[e, base + r] = norm(ref[e, r])
            return carry

        lax.fori_loop(0, 16, step, 0)

    norm_rows(pix, 1 + 8 * c)

    kx_copies = []
    diagonal_copies = []

    def k1_forward(q):
        block = k1x.at[line, pl.ds(3 * q, 3)]

        @pl.when(k1_gets)
        def _():
            arrived(block, r_k1.at[q])

        across = [
            remote(block, block, s_k1.at[d, q], r_k1.at[q], dev(s, x + d, zh, y, c))
            for d in (2, 1, 3)
        ]
        diagonal_copies.extend(across)

        @pl.when(diagonal)
        def _():
            for cpy in across:
                cpy.start()

        for d in (2, 1, 3):
            cpy = remote(
                block, block, s_kx.at[d - 1, q], r_kx.at[d - 1, q],
                dev(s, x + d * (1 - c), zh, y + d * c, c),
            )
            cpy.start()
            kx_copies.append(cpy)

    def wy_wait(lower):
        for core in range(2):

            @pl.when(c == core)
            def _(core=core):
                for dy in range(4):
                    for dc in range(2):
                        if dy or dc:
                            sy = lax.rem(y - dy + 4, 4)
                            sc = core if dc == 0 else 1 - core
                            arrived(
                                wy.at[sy * 2 + sc, PARTS[lower][core]],
                                r_wy.at[lower * 8 + dy * 2 + dc],
                            )

    def packed(a):
        return jnp.concatenate([wy[k, pl.ds(20 * a, 20), :] for k in range(8)], axis=0)

    def at(core, j, z_):
        return wall.at[5 * core + j, rows(z_, SLAB)]

    z1 = lax.rem(zh + way + 4, 4)
    z2 = lax.rem(zh - way + 4, 4)
    z3 = lax.rem(zh + 2, 4)
    zs = (zh, z1, z2, z3)
    chain = []
    shares = []
    side = lax.rem(s + c, 2)

    def share(q, j, n):
        k = len(shares)
        shares.append((q, j, n))
        block = wall.at[pl.ds(5 * c + j, n), rows(zs[q], SLAB)]
        cpy = remote(block, block, s_dd.at[k], r_dd.at[k], partner)
        cpy.start()
        chain.append(cpy)

    def link(q, j, ss, rs, to):
        return remote(at(c, j, zs[q]), at(c, j, zs[q]), ss.at[j], rs.at[j], to)

    def hop1(j):
        arrived(at(c, j, z1), r_h1.at[j])
        cpy = link(1, j, s_h2, r_h2, pair)
        cpy.start()
        chain.append(cpy)

    third = []
    fourth = []

    def hop2(j):
        arrived(at(c, j, z2), r_h2.at[j])
        cpy = link(2, j, s_h3, r_h3, outward)
        goes = side >= 0
        third.append((goes, cpy))

        @pl.when(goes)
        def _():
            cpy.start()

    def hop3(j):
        cpy = link(3, j, s_h4, r_h4, pair)
        comes = side < 0
        fourth.append((comes, cpy))

        @pl.when(comes)
        def _():
            arrived(at(c, j, z3), r_h3.at[j])
            cpy.start()

    def hop4(j):
        arrived(at(c, j, z3), r_h3.at[j])

    def own_slabs(first, count):
        @pl.when(c == 0)
        def _():
            for j in range(first, first + count):
                if j == 0:
                    w = jnp.concatenate([pland[k] for k in range(4)], axis=0)
                else:
                    w = packed(j - 1)
                wall[j, rows(zh, SLAB), :] = w

        @pl.when(c == 1)
        def _():
            for j in range(first, first + count):
                wall[5 + j, rows(zh, SLAB), :] = packed(j)

        for j in range(first, first + count):
            cpy = link(0, j, s_h1, r_h1, outward)
            cpy.start()
            chain.append(cpy)
        share(0, first, count)

    arrived(pxp, r_px)
    norm_rows(pxp, 1 + 8 * other)

    @pl.when(y > 0)
    def _():
        arrived(hal_t, r_ht)
        for e in range(2):
            nb[e, 0] = norm(hal_t[e, 0])

    @pl.when(y == 0)
    def _():
        nb[:, 0] = jnp.zeros((2, 32, D), BF16)

    @pl.when(y < 3)
    def _():
        arrived(hal_b, r_hb)
        for e in range(2):
            nb[e, 17] = norm(hal_b[e, 0])

    @pl.when(y == 3)
    def _():
        nb[:, 17] = jnp.zeros((2, 32, D), BF16)

    k1_forward(0)
    wy_wait(0)
    for dx in range(1, 4):
        arrived(pland.at[lax.rem(x - dx + 4, 4)], r_pr.at[dx - 1])
    own_slabs(0, 2)
    k1_forward(1)

    col = lax.broadcasted_iota(jnp.int32, (D, 256), 1)
    row = lax.broadcasted_iota(jnp.int32, (D, 256), 0)
    want = jnp.where(col < 160, col + lax.div(col, 40) * 120 + zq * 40, -1)
    select = jnp.where(row == want, 1.0, 0.0).astype(BF16)

    def select_rows(i, carry):
        e, b = lax.div(i, 3), lax.rem(i, 3)
        got = dot(nb[e, pl.ds(6 * b, 6)].reshape(192, D), select)
        for r in range(6):
            for h in range(2):
                nsel[h, e, 6 * b + r, pl.ds(8, 32), :] = got[32 * r : 32 * r + 32, 128 * h : 128 * h + 128]
        return carry

    lax.fori_loop(0, 6, select_rows, 0)
    k1_forward(2)

    def box(i, carry):
        e, r = lax.div(i, 9), lax.rem(i, 9)
        for par in range(2):
            for h in range(2):
                v = [
                    nsel[h, e, 2 * r + par, pl.ds(7 + d, 16, stride=2), :]
                    + nsel[h, e, 2 * r + par + 1, pl.ds(7 + d, 16, stride=2), :]
                    for d in range(4)
                ]
                for dx in range(3):
                    both = ((v[dx] + v[dx + 1]) * 0.25).astype(BF16)
                    bq[dx, par, e, r, :, pl.ds(128 * h, 128)] = both
        return carry

    lax.fori_loop(0, 18, box, 0)
    wy_wait(1)
    own_slabs(2, 3)
    hop1(0)

    for q in range(3):
        if q == 2:
            hop1(1)
        for d in range(1, 4):
            arrived(k1x.at[lax.rem(line - d + 4, 4), pl.ds(3 * q, 3)], r_kx.at[d - 1, q])
        for t in range(3 * q, 3 * q + 3):
            dy, dx = t // 3, t % 3
            w = jnp.concatenate([k1x[k, t] for k in range(4)], axis=0)
            a = bq[dx, dy % 2, :, pl.ds(dy // 2, 8), :, :].reshape(256, 256)[:, :160]
            got = dot(a, w)
            if t == 0:
                acc1[...] = got
            else:
                acc1[...] += got
    part[...] = acc1[...].astype(BF16)
    pa_copies = []
    for k in range(1, 4):
        ts = s if k < 2 else 1 - s
        tc = c if k % 2 == 0 else other
        cpy = remote(
            part.at[rows(ts * 2 + tc, 64)], prx.at[k - 1], s_pa.at[k - 1], r_pa.at[k - 1],
            dev(ts, x, zh, y, tc),
        )
        cpy.start()
        pa_copies.append(cpy)
    for i in range(4):
        both = pix[s, 2 * i].astype(F32) + pix[s, 2 * i + 1].astype(F32)
        both = jnp.concatenate([both, jnp.zeros((4, D), F32)], axis=0)
        for b in range(5):
            rtmp[i, b] = both[:, 128 * b : 128 * b + 128]

    hop1(2)
    hop2(0)
    for k in range(3):
        arrived(prx.at[k], r_pa.at[k])
    total = acc1[rows(s * 2 + c, 64), :]
    for k in range(3):
        total += prx[k].astype(F32)
    rest = jnp.concatenate(
        [
            jnp.concatenate(
                [
                    rtmp[i, b, pl.ds(0, 16, stride=2), :] + rtmp[i, b, pl.ds(1, 16, stride=2), :]
                    for b in range(5)
                ],
                axis=1,
            )
            for i in range(4)
        ],
        axis=0,
    )
    pb[...] = (total + rest * 0.25).astype(BF16)

    core = lax.div(x, 2)
    slot = lax.rem(x, 2)
    pl_copies = []
    for dx in (2, 1, 3, 0):
        for dy in (2, 1, 3, 0):
            k = dx * 4 + dy
            cpy = remote(
                pb, plin.at[slot, rows(ch, 64)], s_pl.at[k], r_pl.at[slot * 8 + ch],
                dev(s, x + dx, zh, y + dy, core),
            )
            pl_copies.append(cpy)
            if k:
                cpy.start()

    @pl.when(core != c)
    def _():
        pl_copies[-1].start()

    @pl.when(core == c)
    def _():
        plin[slot, rows(ch, 64), :] = pb[...]

    hop1(3)
    hop2(1)
    hop1(4)
    share(1, 0, 5)
    for j in range(2, 5):
        hop2(j)
    share(2, 0, 5)
    for j in range(5):
        hop3(j)
    hop4(0)
    share(3, 0, 1)

    def shared(k):
        q, j, n = shares[k]
        arrived(wall.at[pl.ds(5 * other + j, n), rows(zs[q], SLAB)], r_dd.at[k])

    for k in (0, 2, 3, 4):
        shared(k)

    pn[...] = jnp.concatenate(
        [wall[0, pl.ds(zb * SLAB + xb * 40, 40), :] for xb in range(4) for zb in range(4)], axis=0
    )
    gain, shift = g2w[:, lanes(x)], s2w[:, lanes(x)]
    inside = lax.rem(lax.broadcasted_iota(jnp.int32, (128, 1), 0), 16) < 14

    def nearest(i):
        return lax.rem(y + i + jnp.where(i == 2, 1, 0) - jnp.where(i == 3, 1, 0), 4)

    def project(i, carry):
        e, m = lax.rem(i, 2), nearest(lax.div(i, 2))
        for k in range(2):
            own = jnp.logical_and(2 * c + e == x, ch == 2 * m + k)

            @pl.when(jnp.logical_not(own))
            def _(k=k):
                arrived(plin.at[e, rows(2 * m + k, 64)], r_pl.at[e * 8 + 2 * m + k])

        p = dot(plin[e, rows(m, 128), :], pn[...]).astype(BF16)
        pjb[e, rows(m, 128), :] = p
        v = jnp.maximum(p.astype(F32) * gain + shift, 0.0)
        v = jnp.where(inside, v, 0.0)
        place = pl.ds(pl.multiple_of(128 * m + 16, 16), 128)
        abuf[0, e, place, :] = pltpu.roll(v, 1, 0).astype(BF16)
        abuf[1, e, place, :] = v.astype(BF16)
        abuf[2, e, place, :] = pltpu.roll(v, 127, 0).astype(BF16)
        return carry

    lax.fori_loop(0, 8, project, 0)

    pj_copies = []
    for e in range(2):
        for tc in range(2):
            own = jnp.logical_and(jnp.logical_and(s == 0, 2 * c + e == x), tc == c)
            src = pjb.at[e, rows(2 * y + tc, 64)]
            cpy = remote(
                src, out.at[s, :, lanes(x)], s_pj.at[2 * e + tc], r_pj.at[4 * s + x],
                dev(0, 2 * c + e, zh, y, tc),
            )
            pj_copies.append((own, cpy))

            @pl.when(jnp.logical_not(own))
            def _(cpy=cpy):
                cpy.start()

            @pl.when(own)
            def _(src=src):
                out[0, :, lanes(x)] = src[...]

    for j in range(1, 5):
        hop4(j)
    share(3, 1, 4)
    for k in (1, 5):
        shared(k)

    adds = x == y

    def c_copy(e, k):
        return remote(
            cp.at[e, rows(k, 64)], cin.at[x * 4 + y], s_c.at[e * 8 + k], r_c.at[x * 4 + y],
            dev(s, 2 * c + e, zh, lax.div(k, 2), lax.rem(k, 2)),
        )

    def c_own(e, k):
        return jnp.logical_and(2 * c + e == x, k == ch)

    def second(i, carry):
        e, m = lax.div(i, 2), lax.rem(i, 2)
        a = jnp.concatenate(
            [
                abuf[t % 3, e, pl.ds(pl.multiple_of(256 * m + 16 * (t // 3), 16), 256), :]
                for t in range(9)
            ],
            axis=1,
        )
        total = dot(a, wall[pl.ds(1, 9)].reshape(9 * D, D))
        proj = pjb[e, rows(m, 256), :].astype(F32)
        cp[e, rows(m, 256), :] = (total + jnp.where(adds, proj, 0.0)).astype(BF16)
        for q in range(4):
            k = 4 * m + q
            own = c_own(e, k)

            @pl.when(jnp.logical_not(own))
            def _(k=k):
                c_copy(e, k).start()

            @pl.when(own)
            def _(k=k):
                cin[x * 4 + y] = cp[e, rows(k, 64), :]

        return carry

    lax.fori_loop(0, 4, second, 0)

    def finish(i, carry):
        yb = nearest(i)
        total = jnp.zeros((64, D), F32)
        for xb in range(4):
            own = jnp.logical_and(jnp.logical_and(core == c, xb == x), yb == y)

            @pl.when(jnp.logical_not(own))
            def _(xb=xb):
                arrived(cin.at[xb * 4 + yb], r_c.at[xb * 4 + yb])

            total += cin[xb * 4 + yb].astype(F32)
        fb[:, lanes(yb)] = total.astype(BF16)

        @pl.when(s == 0)
        def _():
            f_copy(yb).start()

        @pl.when(s == 1)
        def _():
            out[1, :, lanes(yb)] = fb[:, lanes(yb)]

        return carry

    def f_copy(yb):
        block = fb.at[:, lanes(yb)]
        return remote(block, out.at[0, :, lanes(yb)], s_f.at[yb], r_f.at[yb], pair)

    lax.fori_loop(0, 4, finish, 0)

    @pl.when(s == 0)
    def _():
        for sb in range(2):
            for xb in range(4):
                own = jnp.logical_and(jnp.logical_and(sb == 0, xb == x), core == c)

                @pl.when(jnp.logical_not(own))
                def _(sb=sb, xb=xb):
                    arrived(out.at[sb, :, pl.ds(xb * D, D)], r_pj.at[4 * sb + xb])

        for yb in range(4):
            f_copy(yb).wait_send()

    @pl.when(s == 1)
    def _():
        for yb in range(4):
            arrived(out.at[0, :, pl.ds(yb * D, D)], r_f.at[yb])

    for own, cpy in pj_copies:

        @pl.when(jnp.logical_not(own))
        def _(cpy=cpy):
            cpy.wait_send()

    for e in range(2):
        for k in range(8):

            @pl.when(jnp.logical_not(c_own(e, k)))
            def _(e=e, k=k):
                c_copy(e, k).wait_send()

    px_copy.wait_send()

    @pl.when(sends_down)
    def _():
        for cpy in down:
            cpy.wait_send()

    @pl.when(sends_up)
    def _():
        for cpy in up:
            cpy.wait_send()

    @pl.when(k1_sends)
    def _():
        for cpy in k1_copies:
            cpy.wait_send()

    @pl.when(diagonal)
    def _():
        for cpy in diagonal_copies:
            cpy.wait_send()

    for goes, cpy in wy_copies + third + fourth:

        @pl.when(goes)
        def _(cpy=cpy):
            cpy.wait_send()

    @pl.when(core != c)
    def _():
        pl_copies[-1].wait_send()

    for cpy in pr_copies + kx_copies + chain + pa_copies + pl_copies[:-1]:
        cpy.wait_send()


def body(
    pixels,
    first_gain,
    first_shift,
    first_kernel,
    projection,
    second_gain,
    second_shift,
    second_kernel,
):
    dma = pltpu.SemaphoreType.DMA

    def vmem(*shape, dtype=BF16):
        return pltpu.VMEM(shape, dtype)

    counts = [
        (), (), (2,), (), (2,), (), (4, 3), (3,), (3, 3), (3, 3), (3,), (3,), (16,), (16,),
        (5,), (5,), (5,), (5,), (5,), (5,), (5,), (5,), (6,), (6,), (3,), (3,), (16,), (16,),
        (4,), (8,), (16,), (16,), (4,), (4,),
    ]
    result = pl.pallas_call(
        kernel,
        name="window",
        out_shape=jax.ShapeDtypeStruct((2, 64, 4 * D), BF16),
        in_specs=[pl.BlockSpec(memory_space=pltpu.VMEM)] * 8,
        out_specs=pl.BlockSpec(memory_space=pltpu.VMEM),
        scratch_shapes=[
            vmem(2, 8, 28, D),
            vmem(2, 1, 28, D),
            vmem(2, 1, 28, D),
            vmem(2, 112, 4 * D),
            vmem(8, 112, D),
            vmem(4, 40, D),
            vmem(10, D, D),
            vmem(D, D),
            vmem(4, 9, 40, D),
            vmem(2, 18, 32, D),
            vmem(2, 2, 19, 48, 128, dtype=F32),
            vmem(3, 2, 2, 9, 16, 256),
            vmem(256, D, dtype=F32),
            vmem(256, D),
            vmem(3, 64, D),
            vmem(4, 5, 32, 128, dtype=F32),
            vmem(64, D),
            vmem(2, 512, D),
            vmem(2, 512, D),
            vmem(3, 2, 544, D),
            vmem(2, 512, D),
            vmem(16, 64, D),
            vmem(64, 4 * D),
            vmem(1, 4 * D, dtype=F32),
            vmem(1, 4 * D, dtype=F32),
        ]
        + [dma(n) for n in counts],
        compiler_params=pltpu.CompilerParams(
            collective_id=0, has_side_effects=True, vmem_limit_bytes=56 * 2**20
        ),
        cost_estimate=pl.CostEstimate(flops=8 * 10**9, bytes_accessed=10**7, transcendentals=0),
    )(
        pixels,
        first_gain,
        first_shift,
        first_kernel.reshape(9, 40, D),
        projection,
        second_gain,
        second_shift,
        second_kernel.reshape(9, 20, 4 * D),
    )
    return result.reshape(2, 4, 16, 4 * D)[None, :, :, :14]


def solution(mesh):
    placed = (
        P("img", "ch", None, None),
        P(),
        P(),
        P(None, None, "img", None),
        P("img", None),
        P(),
        P(),
        P(None, None, ("img", "ch"), None),
    )
    return jax.shard_map(
        body,
        mesh=mesh,
        in_specs=placed,
        out_specs=P("section", "img", "ch", None, None),
        check_vma=False,
    )
```

```python
import jax
import jax.numpy as jnp
from jax import lax
from jax.experimental import pallas as pl
from jax.experimental.pallas import tpu as pltpu
from jax.sharding import PartitionSpec as P

MESH = pl.DeviceIdType.MESH
F32 = jnp.float32
BF16 = jnp.bfloat16
D = 640
SLAB = 160


PARTS = ((pl.ds(0, 48), pl.ds(0, 48)), (pl.ds(48, 32), pl.ds(48, 64)))


def lanes(i):
    return pl.ds(pl.multiple_of(i * D, 128), D)


def rows(i, n):
    return pl.ds(pl.multiple_of(i * n, 16), n)


def dot(a, b):
    return jnp.dot(a, b, preferred_element_type=F32)


def kernel(
    pix, g1, s1, k1, pr, g2, s2, k2,
    out,
    pxp, hal_t, hal_b, wp, wy, pland, wall, pn, k1x, nb, nsel, bq, acc1, part, prx, rtmp,
    pb, plin, pjb, abuf, cp, cin, fb, g2w, s2w,
    s_px, r_px, s_ht, r_ht, s_hb, r_hb, s_k1, r_k1, s_kx, r_kx, s_pr, r_pr, s_wy, r_wy,
    s_h1, r_h1, s_h2, r_h2, s_h3, r_h3, s_h4, r_h4, s_dd, r_dd, s_pa, r_pa, s_pl, r_pl,
    s_pj, r_pj, s_c, r_c, s_f, r_f,
):
    s = lax.axis_index("section")
    img = lax.axis_index("img")
    ch = lax.axis_index("ch")
    x, zh = lax.div(img, 4), lax.rem(img, 4)
    y, c = lax.div(ch, 2), lax.rem(ch, 2)
    other = 1 - c
    way = 2 * s - 1

    def dev(s_, x_, zh_, y_, c_):
        return (s_, lax.rem(x_ + 8, 4) * 4 + lax.rem(zh_ + 8, 4), lax.rem(y_ + 8, 4) * 2 + c_)

    def remote(src, dst, ss, rs, to):
        return pltpu.make_async_remote_copy(
            src_ref=src, dst_ref=dst, send_sem=ss, recv_sem=rs, device_id=to, device_id_type=MESH
        )

    partner = dev(s, x, zh, y, other)
    pair = dev(1 - s, x, zh, y, c)
    outward = dev(1 - s, x, zh + way, y, c)

    def arrived(dst, rs):
        remote(dst, dst, rs, rs, partner).wait_recv()

    barrier = pltpu.get_barrier_semaphore()
    met = []
    for dx in range(4):
        for dy in range(4):
            for dc in range(2):
                if dx or dy or dc:
                    met.append(dev(s, x + dx, zh, y + dy, c if dc == 0 else other))
    for dx in range(4):
        for dc in range(2):
            met.append(dev(1 - s, x + dx, zh, y, c if dc == 0 else other))
    met.append(outward)
    met.append(dev(1 - s, x, zh + 2, y, c))
    for to in met:
        pl.semaphore_signal(barrier, inc=1, device_id=to, device_id_type=MESH)
    pl.semaphore_wait(barrier, len(met))

    px_copy = remote(pix, pxp, s_px, r_px, partner)
    px_copy.start()
    down = [
        remote(pix.at[:, pl.ds(7, 1)], hal_t, s_ht.at[k], r_ht, dev(s, x, zh, y + 1, k))
        for k in range(2)
    ]
    up = [
        remote(pix.at[:, pl.ds(0, 1)], hal_b, s_hb.at[k], r_hb, dev(s, x, zh, y - 1, k))
        for k in range(2)
    ]
    sends_down = jnp.logical_and(c == 1, y < 3)
    sends_up = jnp.logical_and(c == 0, y > 0)

    @pl.when(sends_down)
    def _():
        for cpy in down:
            cpy.start()

    @pl.when(sends_up)
    def _():
        for cpy in up:
            cpy.start()

    zq_off = (1 - s) * 3 * c + s * (1 + c)
    zq = lax.rem(zh + zq_off, 4)
    line = jnp.where(c == 0, x, y)
    diagonal = jnp.logical_and(c == 1, x == y)
    k1_gets = jnp.logical_not(jnp.logical_and(s == 0, c == 0))
    k1_sends = jnp.logical_or(jnp.logical_and(c == 0, s == 0), diagonal)
    k1_copies = [
        remote(
            k1.at[pl.ds(3 * q, 3)], k1x.at[line, pl.ds(3 * q, 3)], s_k1.at[0, q], r_k1.at[q],
            dev(1 - s, x, zh + s - (1 - s) * (1 + c), y, c),
        )
        for q in range(3)
    ]

    @pl.when(k1_sends)
    def _():
        for cpy in k1_copies:
            cpy.start()

    @pl.when(jnp.logical_not(k1_gets))
    def _():
        k1x[x] = k1[...]

    pr_copies = []
    for dx in range(1, 4):
        to = lax.rem(x + dx, 4)
        cpy = remote(
            pr.at[:, lanes(to)], pland.at[x], s_pr.at[dx - 1], r_pr.at[dx - 1], dev(s, to, zh, y, c)
        )
        cpy.start()
        pr_copies.append(cpy)
    pland[x] = pr[:, lanes(x)]

    wy_copies = []
    for lower in range(2):
        for half, first, count in ((0, 0, 4), (1, 4, 5)):
            for a in range(3 * lower, 3 + 2 * lower):
                if a < count:
                    wp[half, pl.ds(20 * a, 20), :] = k2[first + a]
            if half and lower:
                wp[1, pl.ds(100, 12), :] = jnp.zeros((12, 4 * D), BF16)
        for dy in (2, 1, 3, 0):
            for dc in range(2):
                if dy == 0 and dc == 0:
                    continue
                ty = lax.rem(y + dy, 4)
                tc = c if dc == 0 else other
                k = lower * 8 + dy * 2 + dc
                for core in range(2):
                    part_rows = PARTS[lower][core]
                    cpy = remote(
                        wp.at[core, part_rows, lanes(ty)], wy.at[ch, part_rows],
                        s_wy.at[k], r_wy.at[k], dev(s, x, zh, ty, core),
                    )
                    wy_copies.append((tc == core, cpy))

                    @pl.when(tc == core)
                    def _(cpy=cpy):
                        cpy.start()

    wy[ch, pl.ds(0, 80), :] = wp[c, pl.ds(0, 80), lanes(y)]
    wy[ch, pl.ds(80, 32), :] = wp[1, pl.ds(80, 32), lanes(y)]

    g2w[...] = g2[...].reshape(1, 4 * D)
    s2w[...] = s2[...].reshape(1, 4 * D)
    gain1, shift1 = g1[...].reshape(1, D), s1[...].reshape(1, D)
    nsel[...] = jnp.zeros_like(nsel)
    for k in range(3):
        for e in range(2):
            abuf[k, e, pl.ds(0, 16), :] = jnp.zeros((16, D), BF16)
            abuf[k, e, pl.ds(528, 16), :] = jnp.zeros((16, D), BF16)

    def norm(cells):
        n = jnp.maximum(cells.astype(F32) * gain1 + shift1, 0.0)
        return jnp.concatenate([n, jnp.zeros((4, D), F32)], axis=0).astype(BF16)

    def norm_rows(ref, base):
        def step(i, carry):
            e, r = lax.div(i, 8), lax.rem(i, 8)
            nb[e, base + r] = norm(ref[e, r])
            return carry

        lax.fori_loop(0, 16, step, 0)

    norm_rows(pix, 1 + 8 * c)

    kx_copies = []
    diagonal_copies = []

    def k1_forward(q):
        block = k1x.at[line, pl.ds(3 * q, 3)]

        @pl.when(k1_gets)
        def _():
            arrived(block, r_k1.at[q])

        across = [
            remote(block, block, s_k1.at[d, q], r_k1.at[q], dev(s, x + d, zh, y, c))
            for d in (2, 1, 3)
        ]
        diagonal_copies.extend(across)

        @pl.when(diagonal)
        def _():
            for cpy in across:
                cpy.start()

        for d in (2, 1, 3):
            cpy = remote(
                block, block, s_kx.at[d - 1, q], r_kx.at[d - 1, q],
                dev(s, x + d * (1 - c), zh, y + d * c, c),
            )
            cpy.start()
            kx_copies.append(cpy)

    def wy_wait(lower):
        for core in range(2):

            @pl.when(c == core)
            def _(core=core):
                for dy in range(4):
                    for dc in range(2):
                        if dy or dc:
                            sy = lax.rem(y - dy + 4, 4)
                            sc = core if dc == 0 else 1 - core
                            arrived(
                                wy.at[sy * 2 + sc, PARTS[lower][core]],
                                r_wy.at[lower * 8 + dy * 2 + dc],
                            )

    def packed(a):
        return jnp.concatenate([wy[k, pl.ds(20 * a, 20), :] for k in range(8)], axis=0)

    def at(core, j, z_):
        return wall.at[5 * core + j, rows(z_, SLAB)]

    z1 = lax.rem(zh + way + 4, 4)
    z2 = lax.rem(zh - way + 4, 4)
    z3 = lax.rem(zh + 2, 4)
    zs = (zh, z1, z2, z3)
    chain = []
    shares = []
    side = lax.rem(s + c, 2)

    def share(q, j, n):
        k = len(shares)
        shares.append((q, j, n))
        block = wall.at[pl.ds(5 * c + j, n), rows(zs[q], SLAB)]
        cpy = remote(block, block, s_dd.at[k], r_dd.at[k], partner)
        cpy.start()
        chain.append(cpy)

    def link(q, j, ss, rs, to):
        return remote(at(c, j, zs[q]), at(c, j, zs[q]), ss.at[j], rs.at[j], to)

    def hop1(j):
        arrived(at(c, j, z1), r_h1.at[j])
        cpy = link(1, j, s_h2, r_h2, pair)
        cpy.start()
        chain.append(cpy)

    third = []
    fourth = []

    def hop2(j):
        arrived(at(c, j, z2), r_h2.at[j])
        cpy = link(2, j, s_h3, r_h3, outward)
        goes = side >= 0
        third.append((goes, cpy))

        @pl.when(goes)
        def _():
            cpy.start()

    def hop3(j):
        cpy = link(3, j, s_h4, r_h4, pair)
        comes = side < 0
        fourth.append((comes, cpy))

        @pl.when(comes)
        def _():
            arrived(at(c, j, z3), r_h3.at[j])
            cpy.start()

    def hop4(j):
        arrived(at(c, j, z3), r_h3.at[j])

    def own_slabs(first, count):
        @pl.when(c == 0)
        def _():
            for j in range(first, first + count):
                if j == 0:
                    w = jnp.concatenate([pland[k] for k in range(4)], axis=0)
                else:
                    w = packed(j - 1)
                wall[j, rows(zh, SLAB), :] = w

        @pl.when(c == 1)
        def _():
            for j in range(first, first + count):
                wall[5 + j, rows(zh, SLAB), :] = packed(j)

        for j in range(first, first + count):
            cpy = link(0, j, s_h1, r_h1, outward)
            cpy.start()
            chain.append(cpy)
        share(0, first, count)

    arrived(pxp, r_px)
    norm_rows(pxp, 1 + 8 * other)

    @pl.when(y > 0)
    def _():
        arrived(hal_t, r_ht)
        for e in range(2):
            nb[e, 0] = norm(hal_t[e, 0])

    @pl.when(y == 0)
    def _():
        nb[:, 0] = jnp.zeros((2, 32, D), BF16)

    @pl.when(y < 3)
    def _():
        arrived(hal_b, r_hb)
        for e in range(2):
            nb[e, 17] = norm(hal_b[e, 0])

    @pl.when(y == 3)
    def _():
        nb[:, 17] = jnp.zeros((2, 32, D), BF16)

    k1_forward(0)
    wy_wait(0)
    for dx in range(1, 4):
        arrived(pland.at[lax.rem(x - dx + 4, 4)], r_pr.at[dx - 1])
    own_slabs(0, 2)
    k1_forward(1)

    col = lax.broadcasted_iota(jnp.int32, (D, 256), 1)
    row = lax.broadcasted_iota(jnp.int32, (D, 256), 0)
    want = jnp.where(col < 160, col + lax.div(col, 40) * 120 + zq * 40, -1)
    select = jnp.where(row == want, 1.0, 0.0).astype(BF16)

    def select_rows(i, carry):
        e, b = lax.div(i, 3), lax.rem(i, 3)
        got = dot(nb[e, pl.ds(6 * b, 6)].reshape(192, D), select)
        for r in range(6):
            for h in range(2):
                nsel[h, e, 6 * b + r, pl.ds(8, 32), :] = got[32 * r : 32 * r + 32, 128 * h : 128 * h + 128]
        return carry

    lax.fori_loop(0, 6, select_rows, 0)
    k1_forward(2)

    def box(i, carry):
        e, r = lax.div(i, 9), lax.rem(i, 9)
        for par in range(2):
            for h in range(2):
                v = [
                    nsel[h, e, 2 * r + par, pl.ds(7 + d, 16, stride=2), :]
                    + nsel[h, e, 2 * r + par + 1, pl.ds(7 + d, 16, stride=2), :]
                    for d in range(4)
                ]
                for dx in range(3):
                    both = ((v[dx] + v[dx + 1]) * 0.25).astype(BF16)
                    bq[dx, par, e, r, :, pl.ds(128 * h, 128)] = both
        return carry

    lax.fori_loop(0, 18, box, 0)
    wy_wait(1)
    own_slabs(2, 3)
    hop1(0)

    for q in range(3):
        if q == 2:
            hop1(1)
        for d in range(1, 4):
            arrived(k1x.at[lax.rem(line - d + 4, 4), pl.ds(3 * q, 3)], r_kx.at[d - 1, q])
        for t in range(3 * q, 3 * q + 3):
            dy, dx = t // 3, t % 3
            w = jnp.concatenate([k1x[k, t] for k in range(4)], axis=0)
            a = bq[dx, dy % 2, :, pl.ds(dy // 2, 8), :, :].reshape(256, 256)[:, :160]
            got = dot(a, w)
            if t == 0:
                acc1[...] = got
            else:
                acc1[...] += got
    part[...] = acc1[...].astype(BF16)
    pa_copies = []
    for k in range(1, 4):
        ts = s if k < 2 else 1 - s
        tc = c if k % 2 == 0 else other
        cpy = remote(
            part.at[rows(ts * 2 + tc, 64)], prx.at[k - 1], s_pa.at[k - 1], r_pa.at[k - 1],
            dev(ts, x, zh, y, tc),
        )
        cpy.start()
        pa_copies.append(cpy)
    for i in range(4):
        both = pix[s, 2 * i].astype(F32) + pix[s, 2 * i + 1].astype(F32)
        both = jnp.concatenate([both, jnp.zeros((4, D), F32)], axis=0)
        for b in range(5):
            rtmp[i, b] = both[:, 128 * b : 128 * b + 128]

    hop1(2)
    hop2(0)
    for k in range(3):
        arrived(prx.at[k], r_pa.at[k])
    total = acc1[rows(s * 2 + c, 64), :]
    for k in range(3):
        total += prx[k].astype(F32)
    rest = jnp.concatenate(
        [
            jnp.concatenate(
                [
                    rtmp[i, b, pl.ds(0, 16, stride=2), :] + rtmp[i, b, pl.ds(1, 16, stride=2), :]
                    for b in range(5)
                ],
                axis=1,
            )
            for i in range(4)
        ],
        axis=0,
    )
    pb[...] = (total + rest * 0.25).astype(BF16)

    core = lax.div(x, 2)
    slot = lax.rem(x, 2)
    pl_copies = []
    for dx in (2, 1, 3, 0):
        for dy in (2, 1, 3, 0):
            k = dx * 4 + dy
            cpy = remote(
                pb, plin.at[slot, rows(ch, 64)], s_pl.at[k], r_pl.at[slot * 8 + ch],
                dev(s, x + dx, zh, y + dy, core),
            )
            pl_copies.append(cpy)
            if k:
                cpy.start()

    @pl.when(core != c)
    def _():
        pl_copies[-1].start()

    @pl.when(core == c)
    def _():
        plin[slot, rows(ch, 64), :] = pb[...]

    hop1(3)
    hop2(1)
    hop1(4)
    share(1, 0, 5)
    for j in range(2, 5):
        hop2(j)
    share(2, 0, 5)
    for j in range(5):
        hop3(j)
    hop4(0)
    share(3, 0, 1)

    def shared(k):
        q, j, n = shares[k]
        arrived(wall.at[pl.ds(5 * other + j, n), rows(zs[q], SLAB)], r_dd.at[k])

    for k in (0, 2, 3, 4):
        shared(k)

    pn[...] = jnp.concatenate(
        [wall[0, pl.ds(zb * SLAB + xb * 40, 40), :] for xb in range(4) for zb in range(4)], axis=0
    )
    gain, shift = g2w[:, lanes(x)], s2w[:, lanes(x)]
    inside = lax.rem(lax.broadcasted_iota(jnp.int32, (128, 1), 0), 16) < 14

    def nearest(i):
        return lax.rem(y + i + jnp.where(i == 2, 1, 0) - jnp.where(i == 3, 1, 0), 4)

    def project(i, carry):
        e, m = lax.rem(i, 2), nearest(lax.div(i, 2))
        for k in range(2):
            own = jnp.logical_and(2 * c + e == x, ch == 2 * m + k)

            @pl.when(jnp.logical_not(own))
            def _(k=k):
                arrived(plin.at[e, rows(2 * m + k, 64)], r_pl.at[e * 8 + 2 * m + k])

        p = dot(plin[e, rows(m, 128), :], pn[...]).astype(BF16)
        pjb[e, rows(m, 128), :] = p
        v = jnp.maximum(p.astype(F32) * gain + shift, 0.0)
        v = jnp.where(inside, v, 0.0)
        place = pl.ds(pl.multiple_of(128 * m + 16, 16), 128)
        abuf[0, e, place, :] = pltpu.roll(v, 1, 0).astype(BF16)
        abuf[1, e, place, :] = v.astype(BF16)
        abuf[2, e, place, :] = pltpu.roll(v, 127, 0).astype(BF16)
        return carry

    lax.fori_loop(0, 8, project, 0)

    pj_copies = []
    for e in range(2):
        for tc in range(2):
            own = jnp.logical_and(jnp.logical_and(s == 0, 2 * c + e == x), tc == c)
            src = pjb.at[e, rows(2 * y + tc, 64)]
            cpy = remote(
                src, out.at[s, :, lanes(x)], s_pj.at[2 * e + tc], r_pj.at[4 * s + x],
                dev(0, 2 * c + e, zh, y, tc),
            )
            pj_copies.append((own, cpy))

            @pl.when(jnp.logical_not(own))
            def _(cpy=cpy):
                cpy.start()

            @pl.when(own)
            def _(src=src):
                out[0, :, lanes(x)] = src[...]

    for j in range(1, 5):
        hop4(j)
    share(3, 1, 4)
    for k in (1, 5):
        shared(k)

    adds = x == y

    def c_copy(e, k):
        return remote(
            cp.at[e, rows(k, 64)], cin.at[x * 4 + y], s_c.at[e * 8 + k], r_c.at[x * 4 + y],
            dev(s, 2 * c + e, zh, lax.div(k, 2), lax.rem(k, 2)),
        )

    def c_own(e, k):
        return jnp.logical_and(2 * c + e == x, k == ch)

    def second(i, carry):
        e = lax.rem(lax.div(i, 2) + x, 2)
        m = lax.rem(i + 1 + lax.div(y, 2), 2)
        a = jnp.concatenate(
            [
                abuf[t % 3, e, pl.ds(pl.multiple_of(256 * m + 16 * (t // 3), 16), 256), :]
                for t in range(9)
            ],
            axis=1,
        )
        total = dot(a, wall[pl.ds(1, 9)].reshape(9 * D, D))
        proj = pjb[e, rows(m, 256), :].astype(F32)
        cp[e, rows(m, 256), :] = (total + jnp.where(adds, proj, 0.0)).astype(BF16)
        for q in range(4):
            k = 4 * m + q
            own = c_own(e, k)

            @pl.when(jnp.logical_not(own))
            def _(k=k):
                c_copy(e, k).start()

            @pl.when(own)
            def _(k=k):
                cin[x * 4 + y] = cp[e, rows(k, 64), :]

        return carry

    lax.fori_loop(0, 4, second, 0)

    def finish(i, carry):
        far = 2 * (1 - lax.div(y, 2)) + i
        near = jnp.where(i == 3, y, y + 1 - 2 * lax.rem(y, 2))
        yb = jnp.where(i < 2, far, near)
        total = jnp.zeros((64, D), F32)
        for xb in range(4):
            own = jnp.logical_and(jnp.logical_and(core == c, xb == x), yb == y)

            @pl.when(jnp.logical_not(own))
            def _(xb=xb):
                arrived(cin.at[xb * 4 + yb], r_c.at[xb * 4 + yb])

            total += cin[xb * 4 + yb].astype(F32)
        fb[:, lanes(yb)] = total.astype(BF16)

        @pl.when(s == 0)
        def _():
            f_copy(yb).start()

        @pl.when(s == 1)
        def _():
            out[1, :, lanes(yb)] = fb[:, lanes(yb)]

        return carry

    def f_copy(yb):
        block = fb.at[:, lanes(yb)]
        return remote(block, out.at[0, :, lanes(yb)], s_f.at[yb], r_f.at[yb], pair)

    lax.fori_loop(0, 4, finish, 0)

    @pl.when(s == 0)
    def _():
        for sb in range(2):
            for xb in range(4):
                own = jnp.logical_and(jnp.logical_and(sb == 0, xb == x), core == c)

                @pl.when(jnp.logical_not(own))
                def _(sb=sb, xb=xb):
                    arrived(out.at[sb, :, pl.ds(xb * D, D)], r_pj.at[4 * sb + xb])

        for yb in range(4):
            f_copy(yb).wait_send()

    @pl.when(s == 1)
    def _():
        for yb in range(4):
            arrived(out.at[0, :, pl.ds(yb * D, D)], r_f.at[yb])

    for own, cpy in pj_copies:

        @pl.when(jnp.logical_not(own))
        def _(cpy=cpy):
            cpy.wait_send()

    for e in range(2):
        for k in range(8):

            @pl.when(jnp.logical_not(c_own(e, k)))
            def _(e=e, k=k):
                c_copy(e, k).wait_send()

    px_copy.wait_send()

    @pl.when(sends_down)
    def _():
        for cpy in down:
            cpy.wait_send()

    @pl.when(sends_up)
    def _():
        for cpy in up:
            cpy.wait_send()

    @pl.when(k1_sends)
    def _():
        for cpy in k1_copies:
            cpy.wait_send()

    @pl.when(diagonal)
    def _():
        for cpy in diagonal_copies:
            cpy.wait_send()

    for goes, cpy in wy_copies + third + fourth:

        @pl.when(goes)
        def _(cpy=cpy):
            cpy.wait_send()

    @pl.when(core != c)
    def _():
        pl_copies[-1].wait_send()

    for cpy in pr_copies + kx_copies + chain + pa_copies + pl_copies[:-1]:
        cpy.wait_send()


def body(
    pixels,
    first_gain,
    first_shift,
    first_kernel,
    projection,
    second_gain,
    second_shift,
    second_kernel,
):
    dma = pltpu.SemaphoreType.DMA

    def vmem(*shape, dtype=BF16):
        return pltpu.VMEM(shape, dtype)

    counts = [
        (), (), (2,), (), (2,), (), (4, 3), (3,), (3, 3), (3, 3), (3,), (3,), (16,), (16,),
        (5,), (5,), (5,), (5,), (5,), (5,), (5,), (5,), (6,), (6,), (3,), (3,), (16,), (16,),
        (4,), (8,), (16,), (16,), (4,), (4,),
    ]
    result = pl.pallas_call(
        kernel,
        name="window",
        out_shape=jax.ShapeDtypeStruct((2, 64, 4 * D), BF16),
        in_specs=[pl.BlockSpec(memory_space=pltpu.VMEM)] * 8,
        out_specs=pl.BlockSpec(memory_space=pltpu.VMEM),
        scratch_shapes=[
            vmem(2, 8, 28, D),
            vmem(2, 1, 28, D),
            vmem(2, 1, 28, D),
            vmem(2, 112, 4 * D),
            vmem(8, 112, D),
            vmem(4, 40, D),
            vmem(10, D, D),
            vmem(D, D),
            vmem(4, 9, 40, D),
            vmem(2, 18, 32, D),
            vmem(2, 2, 19, 48, 128, dtype=F32),
            vmem(3, 2, 2, 9, 16, 256),
            vmem(256, D, dtype=F32),
            vmem(256, D),
            vmem(3, 64, D),
            vmem(4, 5, 32, 128, dtype=F32),
            vmem(64, D),
            vmem(2, 512, D),
            vmem(2, 512, D),
            vmem(3, 2, 544, D),
            vmem(2, 512, D),
            vmem(16, 64, D),
            vmem(64, 4 * D),
            vmem(1, 4 * D, dtype=F32),
            vmem(1, 4 * D, dtype=F32),
        ]
        + [dma(n) for n in counts],
        compiler_params=pltpu.CompilerParams(
            collective_id=0, has_side_effects=True, vmem_limit_bytes=56 * 2**20
        ),
        cost_estimate=pl.CostEstimate(flops=8 * 10**9, bytes_accessed=10**7, transcendentals=0),
    )(
        pixels,
        first_gain,
        first_shift,
        first_kernel.reshape(9, 40, D),
        projection,
        second_gain,
        second_shift,
        second_kernel.reshape(9, 20, 4 * D),
    )
    return result.reshape(2, 4, 16, 4 * D)[None, :, :, :14]


def solution(mesh):
    placed = (
        P("img", "ch", None, None),
        P(),
        P(),
        P(None, None, "img", None),
        P("img", None),
        P(),
        P(),
        P(None, None, ("img", "ch"), None),
    )
    return jax.shard_map(
        body,
        mesh=mesh,
        in_specs=placed,
        out_specs=P("section", "img", "ch", None, None),
        check_vma=False,
    )
```

```python
import jax
import jax.numpy as jnp
from jax import lax
from jax.experimental import pallas as pl
from jax.experimental.pallas import tpu as pltpu
from jax.sharding import PartitionSpec as P

MESH = pl.DeviceIdType.MESH
F32 = jnp.float32
BF16 = jnp.bfloat16
D = 640
SLAB = 160


PARTS = ((pl.ds(0, 48), pl.ds(0, 48)), (pl.ds(48, 32), pl.ds(48, 64)))


def lanes(i):
    return pl.ds(pl.multiple_of(i * D, 128), D)


def rows(i, n):
    return pl.ds(pl.multiple_of(i * n, 16), n)


def dot(a, b):
    return jnp.dot(a, b, preferred_element_type=F32)


def kernel(
    pix, g1, s1, k1, pr, g2, s2, k2,
    out,
    pxp, hal_t, hal_b, wp, wy, pland, wall, pn, k1x, nb, nsel, bq, acc1, part, prx, rtmp,
    pb, plin, pjb, abuf, cp, cin, fb, g2w, s2w,
    s_px, r_px, s_ht, r_ht, s_hb, r_hb, s_k1, r_k1, s_kx, r_kx, s_pr, r_pr, s_wy, r_wy,
    s_h1, r_h1, s_h2, r_h2, s_h3, r_h3, s_h4, r_h4, s_dd, r_dd, s_pa, r_pa, s_pl, r_pl,
    s_pj, r_pj, s_c, r_c, s_f, r_f,
):
    s = lax.axis_index("section")
    img = lax.axis_index("img")
    ch = lax.axis_index("ch")
    x, zh = lax.div(img, 4), lax.rem(img, 4)
    y, c = lax.div(ch, 2), lax.rem(ch, 2)
    other = 1 - c
    way = 2 * s - 1

    def dev(s_, x_, zh_, y_, c_):
        return (s_, lax.rem(x_ + 8, 4) * 4 + lax.rem(zh_ + 8, 4), lax.rem(y_ + 8, 4) * 2 + c_)

    def remote(src, dst, ss, rs, to):
        return pltpu.make_async_remote_copy(
            src_ref=src, dst_ref=dst, send_sem=ss, recv_sem=rs, device_id=to, device_id_type=MESH
        )

    partner = dev(s, x, zh, y, other)
    pair = dev(1 - s, x, zh, y, c)
    outward = dev(1 - s, x, zh + way, y, c)

    def arrived(dst, rs):
        remote(dst, dst, rs, rs, partner).wait_recv()

    barrier = pltpu.get_barrier_semaphore()
    met = []
    for dx in range(4):
        for dy in range(4):
            for dc in range(2):
                if dx or dy or dc:
                    met.append(dev(s, x + dx, zh, y + dy, c if dc == 0 else other))
    for dx in range(4):
        for dc in range(2):
            met.append(dev(1 - s, x + dx, zh, y, c if dc == 0 else other))
    met.append(outward)
    met.append(dev(1 - s, x, zh + 2, y, c))
    for to in met:
        pl.semaphore_signal(barrier, inc=1, device_id=to, device_id_type=MESH)
    for half, first, count in ((0, 0, 4), (1, 4, 5)):
        for a in range(count):
            wp[half, pl.ds(20 * a, 20), :] = k2[first + a]
    wp[1, pl.ds(100, 12), :] = jnp.zeros((12, 4 * D), BF16)
    pl.semaphore_wait(barrier, len(met))

    zq_off = (1 - s) * 3 * c + s * (1 + c)
    zq = lax.rem(zh + zq_off, 4)
    line = jnp.where(c == 0, x, y)
    diagonal = jnp.logical_and(c == 1, x == y)
    k1_gets = jnp.logical_not(jnp.logical_and(s == 0, c == 0))
    k1_sends = jnp.logical_or(jnp.logical_and(c == 0, s == 0), diagonal)
    k1_copies = [
        remote(
            k1.at[pl.ds(3 * q, 3)], k1x.at[line, pl.ds(3 * q, 3)], s_k1.at[0, q], r_k1.at[q],
            dev(1 - s, x, zh + s - (1 - s) * (1 + c), y, c),
        )
        for q in range(3)
    ]

    @pl.when(k1_sends)
    def _():
        for cpy in k1_copies:
            cpy.start()

    @pl.when(jnp.logical_not(k1_gets))
    def _():
        k1x[x] = k1[...]

    px_copy = remote(pix, pxp, s_px, r_px, partner)
    px_copy.start()
    down = [
        remote(pix.at[:, pl.ds(7, 1)], hal_t, s_ht.at[k], r_ht, dev(s, x, zh, y + 1, k))
        for k in range(2)
    ]
    up = [
        remote(pix.at[:, pl.ds(0, 1)], hal_b, s_hb.at[k], r_hb, dev(s, x, zh, y - 1, k))
        for k in range(2)
    ]
    sends_down = jnp.logical_and(c == 1, y < 3)
    sends_up = jnp.logical_and(c == 0, y > 0)

    @pl.when(sends_down)
    def _():
        for cpy in down:
            cpy.start()

    @pl.when(sends_up)
    def _():
        for cpy in up:
            cpy.start()

    pr_copies = []
    for dx in range(1, 4):
        to = lax.rem(x + dx, 4)
        cpy = remote(
            pr.at[:, lanes(to)], pland.at[x], s_pr.at[dx - 1], r_pr.at[dx - 1], dev(s, to, zh, y, c)
        )
        cpy.start()
        pr_copies.append(cpy)
    pland[x] = pr[:, lanes(x)]

    wy_copies = []
    for lower in range(2):
        for dy in (2, 1, 3, 0):
            for dc in range(2):
                if dy == 0 and dc == 0:
                    continue
                ty = lax.rem(y + dy, 4)
                tc = c if dc == 0 else other
                k = lower * 8 + dy * 2 + dc
                for core in range(2):
                    part_rows = PARTS[lower][core]
                    cpy = remote(
                        wp.at[core, part_rows, lanes(ty)], wy.at[ch, part_rows],
                        s_wy.at[k], r_wy.at[k], dev(s, x, zh, ty, core),
                    )
                    wy_copies.append((tc == core, cpy))

                    @pl.when(tc == core)
                    def _(cpy=cpy):
                        cpy.start()

    wy[ch, pl.ds(0, 80), :] = wp[c, pl.ds(0, 80), lanes(y)]
    wy[ch, pl.ds(80, 32), :] = wp[1, pl.ds(80, 32), lanes(y)]

    g2w[...] = g2[...].reshape(1, 4 * D)
    s2w[...] = s2[...].reshape(1, 4 * D)
    gain1, shift1 = g1[...].reshape(1, D), s1[...].reshape(1, D)
    nsel[...] = jnp.zeros_like(nsel)
    for k in range(3):
        for e in range(2):
            abuf[k, e, pl.ds(0, 16), :] = jnp.zeros((16, D), BF16)
            abuf[k, e, pl.ds(528, 16), :] = jnp.zeros((16, D), BF16)

    def norm(cells):
        n = jnp.maximum(cells.astype(F32) * gain1 + shift1, 0.0)
        return jnp.concatenate([n, jnp.zeros((4, D), F32)], axis=0).astype(BF16)

    def norm_rows(ref, base):
        def step(i, carry):
            e, r = lax.div(i, 8), lax.rem(i, 8)
            nb[e, base + r] = norm(ref[e, r])
            return carry

        lax.fori_loop(0, 16, step, 0)

    norm_rows(pix, 1 + 8 * c)

    kx_copies = []
    diagonal_copies = []

    def k1_forward(q):
        block = k1x.at[line, pl.ds(3 * q, 3)]

        @pl.when(k1_gets)
        def _():
            arrived(block, r_k1.at[q])

        across = [
            remote(block, block, s_k1.at[d, q], r_k1.at[q], dev(s, x + d, zh, y, c))
            for d in (2, 1, 3)
        ]
        diagonal_copies.extend(across)

        @pl.when(diagonal)
        def _():
            for cpy in across:
                cpy.start()

        for d in (2, 1, 3):
            cpy = remote(
                block, block, s_kx.at[d - 1, q], r_kx.at[d - 1, q],
                dev(s, x + d * (1 - c), zh, y + d * c, c),
            )
            cpy.start()
            kx_copies.append(cpy)

    def wy_wait(lower):
        for core in range(2):

            @pl.when(c == core)
            def _(core=core):
                for dy in range(4):
                    for dc in range(2):
                        if dy or dc:
                            sy = lax.rem(y - dy + 4, 4)
                            sc = core if dc == 0 else 1 - core
                            arrived(
                                wy.at[sy * 2 + sc, PARTS[lower][core]],
                                r_wy.at[lower * 8 + dy * 2 + dc],
                            )

    def packed(a):
        return jnp.concatenate([wy[k, pl.ds(20 * a, 20), :] for k in range(8)], axis=0)

    def at(core, j, z_):
        return wall.at[5 * core + j, rows(z_, SLAB)]

    z1 = lax.rem(zh + way + 4, 4)
    z2 = lax.rem(zh - way + 4, 4)
    z3 = lax.rem(zh + 2, 4)
    zs = (zh, z1, z2, z3)
    chain = []
    shares = []
    side = lax.rem(s + c, 2)

    def share(q, j, n):
        k = len(shares)
        shares.append((q, j, n))
        block = wall.at[pl.ds(5 * c + j, n), rows(zs[q], SLAB)]
        cpy = remote(block, block, s_dd.at[k], r_dd.at[k], partner)
        cpy.start()
        chain.append(cpy)

    def link(q, j, ss, rs, to):
        return remote(at(c, j, zs[q]), at(c, j, zs[q]), ss.at[j], rs.at[j], to)

    def hop1(j):
        arrived(at(c, j, z1), r_h1.at[j])
        cpy = link(1, j, s_h2, r_h2, pair)
        cpy.start()
        chain.append(cpy)

    third = []
    fourth = []

    def hop2(j):
        arrived(at(c, j, z2), r_h2.at[j])
        cpy = link(2, j, s_h3, r_h3, outward)
        goes = side >= 0
        third.append((goes, cpy))

        @pl.when(goes)
        def _():
            cpy.start()

    def hop3(j):
        cpy = link(3, j, s_h4, r_h4, pair)
        comes = side < 0
        fourth.append((comes, cpy))

        @pl.when(comes)
        def _():
            arrived(at(c, j, z3), r_h3.at[j])
            cpy.start()

    def hop4(j):
        arrived(at(c, j, z3), r_h3.at[j])

    def own_slabs(first, count):
        @pl.when(c == 0)
        def _():
            for j in range(first, first + count):
                if j == 0:
                    w = jnp.concatenate([pland[k] for k in range(4)], axis=0)
                else:
                    w = packed(j - 1)
                wall[j, rows(zh, SLAB), :] = w

        @pl.when(c == 1)
        def _():
            for j in range(first, first + count):
                wall[5 + j, rows(zh, SLAB), :] = packed(j)

        for j in range(first, first + count):
            cpy = link(0, j, s_h1, r_h1, outward)
            cpy.start()
            chain.append(cpy)
        share(0, first, count)

    arrived(pxp, r_px)
    norm_rows(pxp, 1 + 8 * other)

    @pl.when(y > 0)
    def _():
        arrived(hal_t, r_ht)
        for e in range(2):
            nb[e, 0] = norm(hal_t[e, 0])

    @pl.when(y == 0)
    def _():
        nb[:, 0] = jnp.zeros((2, 32, D), BF16)

    @pl.when(y < 3)
    def _():
        arrived(hal_b, r_hb)
        for e in range(2):
            nb[e, 17] = norm(hal_b[e, 0])

    @pl.when(y == 3)
    def _():
        nb[:, 17] = jnp.zeros((2, 32, D), BF16)

    k1_forward(0)
    wy_wait(0)
    for dx in range(1, 4):
        arrived(pland.at[lax.rem(x - dx + 4, 4)], r_pr.at[dx - 1])
    own_slabs(0, 2)
    k1_forward(1)

    col = lax.broadcasted_iota(jnp.int32, (D, 256), 1)
    row = lax.broadcasted_iota(jnp.int32, (D, 256), 0)
    want = jnp.where(col < 160, col + lax.div(col, 40) * 120 + zq * 40, -1)
    select = jnp.where(row == want, 1.0, 0.0).astype(BF16)

    def select_rows(i, carry):
        e, b = lax.div(i, 3), lax.rem(i, 3)
        got = dot(nb[e, pl.ds(6 * b, 6)].reshape(192, D), select)
        for r in range(6):
            for h in range(2):
                nsel[h, e, 6 * b + r, pl.ds(8, 32), :] = got[32 * r : 32 * r + 32, 128 * h : 128 * h + 128]
        return carry

    lax.fori_loop(0, 6, select_rows, 0)
    k1_forward(2)

    def box(i, carry):
        e, r = lax.div(i, 9), lax.rem(i, 9)
        for par in range(2):
            for h in range(2):
                v = [
                    nsel[h, e, 2 * r + par, pl.ds(7 + d, 16, stride=2), :]
                    + nsel[h, e, 2 * r + par + 1, pl.ds(7 + d, 16, stride=2), :]
                    for d in range(4)
                ]
                for dx in range(3):
                    both = ((v[dx] + v[dx + 1]) * 0.25).astype(BF16)
                    bq[dx, par, e, r, :, pl.ds(128 * h, 128)] = both
        return carry

    lax.fori_loop(0, 18, box, 0)
    wy_wait(1)
    own_slabs(2, 3)
    hop1(0)

    for q in range(3):
        if q == 2:
            hop1(1)
        for d in range(1, 4):
            arrived(k1x.at[lax.rem(line - d + 4, 4), pl.ds(3 * q, 3)], r_kx.at[d - 1, q])
        for t in range(3 * q, 3 * q + 3):
            dy, dx = t // 3, t % 3
            w = jnp.concatenate([k1x[k, t] for k in range(4)], axis=0)
            a = bq[dx, dy % 2, :, pl.ds(dy // 2, 8), :, :].reshape(256, 256)[:, :160]
            got = dot(a, w)
            if t == 0:
                acc1[...] = got
            else:
                acc1[...] += got
    part[...] = acc1[...].astype(BF16)
    pa_copies = []
    for k in range(1, 4):
        ts = s if k < 2 else 1 - s
        tc = c if k % 2 == 0 else other
        cpy = remote(
            part.at[rows(ts * 2 + tc, 64)], prx.at[k - 1], s_pa.at[k - 1], r_pa.at[k - 1],
            dev(ts, x, zh, y, tc),
        )
        cpy.start()
        pa_copies.append(cpy)
    for i in range(4):
        both = pix[s, 2 * i].astype(F32) + pix[s, 2 * i + 1].astype(F32)
        both = jnp.concatenate([both, jnp.zeros((4, D), F32)], axis=0)
        for b in range(5):
            rtmp[i, b] = both[:, 128 * b : 128 * b + 128]

    hop1(2)
    hop2(0)
    for k in range(3):
        arrived(prx.at[k], r_pa.at[k])
    total = acc1[rows(s * 2 + c, 64), :]
    for k in range(3):
        total += prx[k].astype(F32)
    rest = jnp.concatenate(
        [
            jnp.concatenate(
                [
                    rtmp[i, b, pl.ds(0, 16, stride=2), :] + rtmp[i, b, pl.ds(1, 16, stride=2), :]
                    for b in range(5)
                ],
                axis=1,
            )
            for i in range(4)
        ],
        axis=0,
    )
    pb[...] = (total + rest * 0.25).astype(BF16)

    core = lax.div(x, 2)
    slot = lax.rem(x, 2)
    pl_copies = []
    for dx in (2, 1, 3, 0):
        for dy in (2, 1, 3, 0):
            k = dx * 4 + dy
            cpy = remote(
                pb, plin.at[slot, rows(ch, 64)], s_pl.at[k], r_pl.at[slot * 8 + ch],
                dev(s, x + dx, zh, y + dy, core),
            )
            pl_copies.append(cpy)
            if k:
                cpy.start()

    @pl.when(core != c)
    def _():
        pl_copies[-1].start()

    @pl.when(core == c)
    def _():
        plin[slot, rows(ch, 64), :] = pb[...]

    hop1(3)
    hop2(1)
    hop1(4)
    share(1, 0, 5)
    for j in range(2, 5):
        hop2(j)
    share(2, 0, 5)
    for j in range(5):
        hop3(j)
    hop4(0)
    share(3, 0, 1)

    def shared(k):
        q, j, n = shares[k]
        arrived(wall.at[pl.ds(5 * other + j, n), rows(zs[q], SLAB)], r_dd.at[k])

    for k in (0, 2, 3, 4):
        shared(k)

    pn[...] = jnp.concatenate(
        [wall[0, pl.ds(zb * SLAB + xb * 40, 40), :] for xb in range(4) for zb in range(4)], axis=0
    )
    gain, shift = g2w[:, lanes(x)], s2w[:, lanes(x)]
    inside = lax.rem(lax.broadcasted_iota(jnp.int32, (128, 1), 0), 16) < 14

    def nearest(i):
        return lax.rem(y + i + jnp.where(i == 2, 1, 0) - jnp.where(i == 3, 1, 0), 4)

    def project(i, carry):
        e, m = lax.rem(i, 2), nearest(lax.div(i, 2))
        for k in range(2):
            own = jnp.logical_and(2 * c + e == x, ch == 2 * m + k)

            @pl.when(jnp.logical_not(own))
            def _(k=k):
                arrived(plin.at[e, rows(2 * m + k, 64)], r_pl.at[e * 8 + 2 * m + k])

        p = dot(plin[e, rows(m, 128), :], pn[...]).astype(BF16)
        pjb[e, rows(m, 128), :] = p
        v = jnp.maximum(p.astype(F32) * gain + shift, 0.0)
        v = jnp.where(inside, v, 0.0)
        place = pl.ds(pl.multiple_of(128 * m + 16, 16), 128)
        abuf[0, e, place, :] = pltpu.roll(v, 1, 0).astype(BF16)
        abuf[1, e, place, :] = v.astype(BF16)
        abuf[2, e, place, :] = pltpu.roll(v, 127, 0).astype(BF16)
        return carry

    lax.fori_loop(0, 8, project, 0)

    pj_copies = []
    for e in range(2):
        for tc in range(2):
            own = jnp.logical_and(jnp.logical_and(s == 0, 2 * c + e == x), tc == c)
            src = pjb.at[e, rows(2 * y + tc, 64)]
            cpy = remote(
                src, out.at[s, :, lanes(x)], s_pj.at[2 * e + tc], r_pj.at[4 * s + x],
                dev(0, 2 * c + e, zh, y, tc),
            )
            pj_copies.append((own, cpy))

            @pl.when(jnp.logical_not(own))
            def _(cpy=cpy):
                cpy.start()

            @pl.when(own)
            def _(src=src):
                out[0, :, lanes(x)] = src[...]

    for j in range(1, 5):
        hop4(j)
    share(3, 1, 4)
    for k in (1, 5):
        shared(k)

    adds = x == y

    def c_copy(e, k):
        return remote(
            cp.at[e, rows(k, 64)], cin.at[x * 4 + y], s_c.at[e * 8 + k], r_c.at[x * 4 + y],
            dev(s, 2 * c + e, zh, lax.div(k, 2), lax.rem(k, 2)),
        )

    def c_own(e, k):
        return jnp.logical_and(2 * c + e == x, k == ch)

    def second(i, carry):
        e = lax.rem(lax.div(i, 2) + x, 2)
        m = lax.rem(i + 1 + lax.div(y, 2), 2)
        a = jnp.concatenate(
            [
                abuf[t % 3, e, pl.ds(pl.multiple_of(256 * m + 16 * (t // 3), 16), 256), :]
                for t in range(9)
            ],
            axis=1,
        )
        total = dot(a, wall[pl.ds(1, 9)].reshape(9 * D, D))
        proj = pjb[e, rows(m, 256), :].astype(F32)
        cp[e, rows(m, 256), :] = (total + jnp.where(adds, proj, 0.0)).astype(BF16)
        for q in range(4):
            k = 4 * m + q
            own = c_own(e, k)

            @pl.when(jnp.logical_not(own))
            def _(k=k):
                c_copy(e, k).start()

            @pl.when(own)
            def _(k=k):
                cin[x * 4 + y] = cp[e, rows(k, 64), :]

        return carry

    lax.fori_loop(0, 4, second, 0)

    def finish(i, carry):
        far = 2 * (1 - lax.div(y, 2)) + i
        near = jnp.where(i == 3, y, y + 1 - 2 * lax.rem(y, 2))
        yb = jnp.where(i < 2, far, near)
        total = jnp.zeros((64, D), F32)
        for xb in range(4):
            own = jnp.logical_and(jnp.logical_and(core == c, xb == x), yb == y)

            @pl.when(jnp.logical_not(own))
            def _(xb=xb):
                arrived(cin.at[xb * 4 + yb], r_c.at[xb * 4 + yb])

            total += cin[xb * 4 + yb].astype(F32)
        fb[:, lanes(yb)] = total.astype(BF16)

        @pl.when(s == 0)
        def _():
            f_copy(yb).start()

        @pl.when(s == 1)
        def _():
            out[1, :, lanes(yb)] = fb[:, lanes(yb)]

        return carry

    def f_copy(yb):
        block = fb.at[:, lanes(yb)]
        return remote(block, out.at[0, :, lanes(yb)], s_f.at[yb], r_f.at[yb], pair)

    lax.fori_loop(0, 4, finish, 0)

    @pl.when(s == 0)
    def _():
        for sb in range(2):
            for xb in range(4):
                own = jnp.logical_and(jnp.logical_and(sb == 0, xb == x), core == c)

                @pl.when(jnp.logical_not(own))
                def _(sb=sb, xb=xb):
                    arrived(out.at[sb, :, pl.ds(xb * D, D)], r_pj.at[4 * sb + xb])

        for yb in range(4):
            f_copy(yb).wait_send()

    @pl.when(s == 1)
    def _():
        for yb in range(4):
            arrived(out.at[0, :, pl.ds(yb * D, D)], r_f.at[yb])

    for own, cpy in pj_copies:

        @pl.when(jnp.logical_not(own))
        def _(cpy=cpy):
            cpy.wait_send()

    for e in range(2):
        for k in range(8):

            @pl.when(jnp.logical_not(c_own(e, k)))
            def _(e=e, k=k):
                c_copy(e, k).wait_send()

    px_copy.wait_send()

    @pl.when(sends_down)
    def _():
        for cpy in down:
            cpy.wait_send()

    @pl.when(sends_up)
    def _():
        for cpy in up:
            cpy.wait_send()

    @pl.when(k1_sends)
    def _():
        for cpy in k1_copies:
            cpy.wait_send()

    @pl.when(diagonal)
    def _():
        for cpy in diagonal_copies:
            cpy.wait_send()

    for goes, cpy in wy_copies + third + fourth:

        @pl.when(goes)
        def _(cpy=cpy):
            cpy.wait_send()

    @pl.when(core != c)
    def _():
        pl_copies[-1].wait_send()

    for cpy in pr_copies + kx_copies + chain + pa_copies + pl_copies[:-1]:
        cpy.wait_send()


def body(
    pixels,
    first_gain,
    first_shift,
    first_kernel,
    projection,
    second_gain,
    second_shift,
    second_kernel,
):
    dma = pltpu.SemaphoreType.DMA

    def vmem(*shape, dtype=BF16):
        return pltpu.VMEM(shape, dtype)

    counts = [
        (), (), (2,), (), (2,), (), (4, 3), (3,), (3, 3), (3, 3), (3,), (3,), (16,), (16,),
        (5,), (5,), (5,), (5,), (5,), (5,), (5,), (5,), (6,), (6,), (3,), (3,), (16,), (16,),
        (4,), (8,), (16,), (16,), (4,), (4,),
    ]
    result = pl.pallas_call(
        kernel,
        name="window",
        out_shape=jax.ShapeDtypeStruct((2, 64, 4 * D), BF16),
        in_specs=[pl.BlockSpec(memory_space=pltpu.VMEM)] * 8,
        out_specs=pl.BlockSpec(memory_space=pltpu.VMEM),
        scratch_shapes=[
            vmem(2, 8, 28, D),
            vmem(2, 1, 28, D),
            vmem(2, 1, 28, D),
            vmem(2, 112, 4 * D),
            vmem(8, 112, D),
            vmem(4, 40, D),
            vmem(10, D, D),
            vmem(D, D),
            vmem(4, 9, 40, D),
            vmem(2, 18, 32, D),
            vmem(2, 2, 19, 48, 128, dtype=F32),
            vmem(3, 2, 2, 9, 16, 256),
            vmem(256, D, dtype=F32),
            vmem(256, D),
            vmem(3, 64, D),
            vmem(4, 5, 32, 128, dtype=F32),
            vmem(64, D),
            vmem(2, 512, D),
            vmem(2, 512, D),
            vmem(3, 2, 544, D),
            vmem(2, 512, D),
            vmem(16, 64, D),
            vmem(64, 4 * D),
            vmem(1, 4 * D, dtype=F32),
            vmem(1, 4 * D, dtype=F32),
        ]
        + [dma(n) for n in counts],
        compiler_params=pltpu.CompilerParams(
            collective_id=0, has_side_effects=True, vmem_limit_bytes=56 * 2**20
        ),
        cost_estimate=pl.CostEstimate(flops=8 * 10**9, bytes_accessed=10**7, transcendentals=0),
    )(
        pixels,
        first_gain,
        first_shift,
        first_kernel.reshape(9, 40, D),
        projection,
        second_gain,
        second_shift,
        second_kernel.reshape(9, 20, 4 * D),
    )
    return result.reshape(2, 4, 16, 4 * D)[None, :, :, :14]


def solution(mesh):
    placed = (
        P("img", "ch", None, None),
        P(),
        P(),
        P(None, None, "img", None),
        P("img", None),
        P(),
        P(),
        P(None, None, ("img", "ch"), None),
    )
    return jax.shard_map(
        body,
        mesh=mesh,
        in_specs=placed,
        out_specs=P("section", "img", "ch", None, None),
        check_vma=False,
    )
```

```python
import jax
import jax.numpy as jnp
from jax import lax
from jax.experimental import pallas as pl
from jax.experimental.pallas import tpu as pltpu
from jax.sharding import PartitionSpec as P

MESH = pl.DeviceIdType.MESH
F32 = jnp.float32
BF16 = jnp.bfloat16
D = 640
SLAB = 160


PARTS = ((pl.ds(0, 48), pl.ds(0, 48)), (pl.ds(48, 32), pl.ds(48, 64)))


def lanes(i):
    return pl.ds(pl.multiple_of(i * D, 128), D)


def rows(i, n):
    return pl.ds(pl.multiple_of(i * n, 16), n)


def dot(a, b):
    return jnp.dot(a, b, preferred_element_type=F32)


def kernel(
    pix, g1, s1, k1, pr, g2, s2, k2,
    out,
    pxp, hal_t, hal_b, wp, wy, pland, wall, pn, k1x, nb, nsel, bq, acc1, part, prx, rtmp,
    pb, plin, pjb, abuf, cp, cin, fb, g2w, s2w,
    s_px, r_px, s_ht, r_ht, s_hb, r_hb, s_k1, r_k1, s_kx, r_kx, s_pr, r_pr, s_wy, r_wy,
    s_h1, r_h1, s_h2, r_h2, s_h3, r_h3, s_h4, r_h4, s_dd, r_dd, s_pa, r_pa, s_pl, r_pl,
    s_pj, r_pj, s_c, r_c, s_f, r_f,
):
    s = lax.axis_index("section")
    img = lax.axis_index("img")
    ch = lax.axis_index("ch")
    x, zh = lax.div(img, 4), lax.rem(img, 4)
    y, c = lax.div(ch, 2), lax.rem(ch, 2)
    other = 1 - c
    way = 2 * s - 1

    def dev(s_, x_, zh_, y_, c_):
        return (s_, lax.rem(x_ + 8, 4) * 4 + lax.rem(zh_ + 8, 4), lax.rem(y_ + 8, 4) * 2 + c_)

    def remote(src, dst, ss, rs, to):
        return pltpu.make_async_remote_copy(
            src_ref=src, dst_ref=dst, send_sem=ss, recv_sem=rs, device_id=to, device_id_type=MESH
        )

    partner = dev(s, x, zh, y, other)
    pair = dev(1 - s, x, zh, y, c)
    outward = dev(1 - s, x, zh + way, y, c)

    def arrived(dst, rs):
        remote(dst, dst, rs, rs, partner).wait_recv()

    barrier = pltpu.get_barrier_semaphore()
    met = []
    for dx in range(4):
        for dy in range(4):
            for dc in range(2):
                if dx or dy or dc:
                    met.append(dev(s, x + dx, zh, y + dy, c if dc == 0 else other))
    for dx in range(4):
        for dc in range(2):
            met.append(dev(1 - s, x + dx, zh, y, c if dc == 0 else other))
    met.append(outward)
    met.append(dev(1 - s, x, zh + 2, y, c))
    for to in met:
        pl.semaphore_signal(barrier, inc=1, device_id=to, device_id_type=MESH)
    pl.semaphore_wait(barrier, len(met))

    px_copy = remote(pix, pxp, s_px, r_px, partner)
    px_copy.start()
    down = [
        remote(pix.at[:, pl.ds(7, 1)], hal_t, s_ht.at[k], r_ht, dev(s, x, zh, y + 1, k))
        for k in range(2)
    ]
    up = [
        remote(pix.at[:, pl.ds(0, 1)], hal_b, s_hb.at[k], r_hb, dev(s, x, zh, y - 1, k))
        for k in range(2)
    ]
    sends_down = jnp.logical_and(c == 1, y < 3)
    sends_up = jnp.logical_and(c == 0, y > 0)

    @pl.when(sends_down)
    def _():
        for cpy in down:
            cpy.start()

    @pl.when(sends_up)
    def _():
        for cpy in up:
            cpy.start()

    zq_off = (1 - s) * 3 * c + s * (1 + c)
    zq = lax.rem(zh + zq_off, 4)
    line = jnp.where(c == 0, x, y)
    diagonal = jnp.logical_and(c == 1, x == y)
    k1_gets = jnp.logical_not(jnp.logical_and(s == 0, c == 0))
    k1_sends = jnp.logical_or(jnp.logical_and(c == 0, s == 0), diagonal)
    k1_copies = [
        remote(
            k1.at[pl.ds(3 * q, 3)], k1x.at[line, pl.ds(3 * q, 3)], s_k1.at[0, q], r_k1.at[q],
            dev(1 - s, x, zh + s - (1 - s) * (1 + c), y, c),
        )
        for q in range(3)
    ]

    @pl.when(k1_sends)
    def _():
        for cpy in k1_copies:
            cpy.start()

    @pl.when(jnp.logical_not(k1_gets))
    def _():
        k1x[x] = k1[...]

    pr_copies = []
    for dx in range(1, 4):
        to = lax.rem(x + dx, 4)
        cpy = remote(
            pr.at[:, lanes(to)], pland.at[x], s_pr.at[dx - 1], r_pr.at[dx - 1], dev(s, to, zh, y, c)
        )
        cpy.start()
        pr_copies.append(cpy)
    pland[x] = pr[:, lanes(x)]

    wy_copies = []
    for lower in range(2):
        for half, first, count in ((0, 0, 4), (1, 4, 5)):
            for a in range(3 * lower, 3 + 2 * lower):
                if a < count:
                    wp[half, pl.ds(20 * a, 20), :] = k2[first + a]
            if half and lower:
                wp[1, pl.ds(100, 12), :] = jnp.zeros((12, 4 * D), BF16)
        for dy in (2, 1, 3, 0):
            for dc in range(2):
                if dy == 0 and dc == 0:
                    continue
                ty = lax.rem(y + dy, 4)
                tc = c if dc == 0 else other
                k = lower * 8 + dy * 2 + dc
                for core in range(2):
                    part_rows = PARTS[lower][core]
                    cpy = remote(
                        wp.at[core, part_rows, lanes(ty)], wy.at[ch, part_rows],
                        s_wy.at[k], r_wy.at[k], dev(s, x, zh, ty, core),
                    )
                    wy_copies.append((tc == core, cpy))

                    @pl.when(tc == core)
                    def _(cpy=cpy):
                        cpy.start()

    wy[ch, pl.ds(0, 80), :] = wp[c, pl.ds(0, 80), lanes(y)]
    wy[ch, pl.ds(80, 32), :] = wp[1, pl.ds(80, 32), lanes(y)]

    g2w[...] = g2[...].reshape(1, 4 * D)
    s2w[...] = s2[...].reshape(1, 4 * D)
    gain1, shift1 = g1[...].reshape(1, D), s1[...].reshape(1, D)
    nsel[...] = jnp.zeros_like(nsel)
    for k in range(3):
        for e in range(2):
            abuf[k, e, pl.ds(0, 16), :] = jnp.zeros((16, D), BF16)
            abuf[k, e, pl.ds(528, 16), :] = jnp.zeros((16, D), BF16)

    def norm(cells):
        n = jnp.maximum(cells.astype(F32) * gain1 + shift1, 0.0)
        return jnp.concatenate([n, jnp.zeros((4, D), F32)], axis=0).astype(BF16)

    def norm_rows(ref, base):
        def step(i, carry):
            e, r = lax.div(i, 8), lax.rem(i, 8)
            nb[e, base + r] = norm(ref[e, r])
            return carry

        lax.fori_loop(0, 16, step, 0)

    norm_rows(pix, 1 + 8 * c)

    kx_copies = []
    diagonal_copies = []

    def k1_forward(q):
        block = k1x.at[line, pl.ds(3 * q, 3)]

        @pl.when(k1_gets)
        def _():
            arrived(block, r_k1.at[q])

        across = [
            remote(block, block, s_k1.at[d, q], r_k1.at[q], dev(s, x + d, zh, y, c))
            for d in (2, 1, 3)
        ]
        diagonal_copies.extend(across)

        @pl.when(diagonal)
        def _():
            for cpy in across:
                cpy.start()

        for d in (2, 1, 3):
            cpy = remote(
                block, block, s_kx.at[d - 1, q], r_kx.at[d - 1, q],
                dev(s, x + d * (1 - c), zh, y + d * c, c),
            )
            cpy.start()
            kx_copies.append(cpy)

    def wy_wait(lower):
        for core in range(2):

            @pl.when(c == core)
            def _(core=core):
                for dy in range(4):
                    for dc in range(2):
                        if dy or dc:
                            sy = lax.rem(y - dy + 4, 4)
                            sc = core if dc == 0 else 1 - core
                            arrived(
                                wy.at[sy * 2 + sc, PARTS[lower][core]],
                                r_wy.at[lower * 8 + dy * 2 + dc],
                            )

    def packed(a):
        return jnp.concatenate([wy[k, pl.ds(20 * a, 20), :] for k in range(8)], axis=0)

    def at(core, j, z_):
        return wall.at[5 * core + j, rows(z_, SLAB)]

    z1 = lax.rem(zh + way + 4, 4)
    z2 = lax.rem(zh - way + 4, 4)
    z3 = lax.rem(zh + 2, 4)
    zs = (zh, z1, z2, z3)
    chain = []
    shares = []
    side = lax.rem(s + c, 2)

    def share(q, j, n):
        k = len(shares)
        shares.append((q, j, n))
        block = wall.at[pl.ds(5 * c + j, n), rows(zs[q], SLAB)]
        cpy = remote(block, block, s_dd.at[k], r_dd.at[k], partner)
        cpy.start()
        chain.append(cpy)

    def link(q, j, ss, rs, to):
        return remote(at(c, j, zs[q]), at(c, j, zs[q]), ss.at[j], rs.at[j], to)

    def hop1(j):
        arrived(at(c, j, z1), r_h1.at[j])
        cpy = link(1, j, s_h2, r_h2, pair)
        cpy.start()
        chain.append(cpy)

    third = []
    fourth = []

    def hop2(j):
        arrived(at(c, j, z2), r_h2.at[j])
        cpy = link(2, j, s_h3, r_h3, outward)
        goes = side >= 0
        third.append((goes, cpy))

        @pl.when(goes)
        def _():
            cpy.start()

    def hop3(j):
        cpy = link(3, j, s_h4, r_h4, pair)
        comes = side < 0
        fourth.append((comes, cpy))

        @pl.when(comes)
        def _():
            arrived(at(c, j, z3), r_h3.at[j])
            cpy.start()

    def hop4(j):
        arrived(at(c, j, z3), r_h3.at[j])

    def own_slabs(first, count):
        @pl.when(c == 0)
        def _():
            for j in range(first, first + count):
                if j == 0:
                    w = jnp.concatenate([pland[k] for k in range(4)], axis=0)
                else:
                    w = packed(j - 1)
                wall[j, rows(zh, SLAB), :] = w

        @pl.when(c == 1)
        def _():
            for j in range(first, first + count):
                wall[5 + j, rows(zh, SLAB), :] = packed(j)

        for j in range(first, first + count):
            cpy = link(0, j, s_h1, r_h1, outward)
            cpy.start()
            chain.append(cpy)
        share(0, first, count)

    arrived(pxp, r_px)
    norm_rows(pxp, 1 + 8 * other)

    @pl.when(y > 0)
    def _():
        arrived(hal_t, r_ht)
        for e in range(2):
            nb[e, 0] = norm(hal_t[e, 0])

    @pl.when(y == 0)
    def _():
        nb[:, 0] = jnp.zeros((2, 32, D), BF16)

    @pl.when(y < 3)
    def _():
        arrived(hal_b, r_hb)
        for e in range(2):
            nb[e, 17] = norm(hal_b[e, 0])

    @pl.when(y == 3)
    def _():
        nb[:, 17] = jnp.zeros((2, 32, D), BF16)

    k1_forward(0)
    wy_wait(0)
    for dx in range(1, 4):
        arrived(pland.at[lax.rem(x - dx + 4, 4)], r_pr.at[dx - 1])
    own_slabs(0, 2)
    k1_forward(1)

    col = lax.broadcasted_iota(jnp.int32, (D, 256), 1)
    row = lax.broadcasted_iota(jnp.int32, (D, 256), 0)
    want = jnp.where(col < 160, col + lax.div(col, 40) * 120 + zq * 40, -1)
    select = jnp.where(row == want, 1.0, 0.0).astype(BF16)

    def select_rows(i, carry):
        e, b = lax.div(i, 3), lax.rem(i, 3)
        got = dot(nb[e, pl.ds(6 * b, 6)].reshape(192, D), select)
        for r in range(6):
            for h in range(2):
                nsel[h, e, 6 * b + r, pl.ds(8, 32), :] = got[32 * r : 32 * r + 32, 128 * h : 128 * h + 128]
        return carry

    lax.fori_loop(0, 6, select_rows, 0)
    k1_forward(2)

    def box(i, carry):
        e, r = lax.div(i, 9), lax.rem(i, 9)
        for par in range(2):
            for h in range(2):
                v = [
                    nsel[h, e, 2 * r + par, pl.ds(7 + d, 16, stride=2), :]
                    + nsel[h, e, 2 * r + par + 1, pl.ds(7 + d, 16, stride=2), :]
                    for d in range(4)
                ]
                for dx in range(3):
                    both = ((v[dx] + v[dx + 1]) * 0.25).astype(BF16)
                    bq[dx, par, e, r, :, pl.ds(128 * h, 128)] = both
        return carry

    lax.fori_loop(0, 18, box, 0)
    wy_wait(1)
    own_slabs(2, 3)
    hop1(0)

    for q in range(3):
        if q == 2:
            hop1(1)
        for d in range(1, 4):
            arrived(k1x.at[lax.rem(line - d + 4, 4), pl.ds(3 * q, 3)], r_kx.at[d - 1, q])
        for t in range(3 * q, 3 * q + 3):
            dy, dx = t // 3, t % 3
            w = jnp.concatenate([k1x[k, t] for k in range(4)], axis=0)
            a = bq[dx, dy % 2, :, pl.ds(dy // 2, 8), :, :].reshape(256, 256)[:, :160]
            got = dot(a, w)
            if t == 0:
                acc1[...] = got
            else:
                acc1[...] += got
    part[...] = acc1[...].astype(BF16)
    pa_copies = []
    for k in range(1, 4):
        ts = s if k < 2 else 1 - s
        tc = c if k % 2 == 0 else other
        cpy = remote(
            part.at[rows(ts * 2 + tc, 64)], prx.at[k - 1], s_pa.at[k - 1], r_pa.at[k - 1],
            dev(ts, x, zh, y, tc),
        )
        cpy.start()
        pa_copies.append(cpy)
    for i in range(4):
        both = pix[s, 2 * i].astype(F32) + pix[s, 2 * i + 1].astype(F32)
        both = jnp.concatenate([both, jnp.zeros((4, D), F32)], axis=0)
        for b in range(5):
            rtmp[i, b] = both[:, 128 * b : 128 * b + 128]

    hop1(2)
    hop2(0)
    for k in range(3):
        arrived(prx.at[k], r_pa.at[k])
    total = acc1[rows(s * 2 + c, 64), :]
    for k in range(3):
        total += prx[k].astype(F32)
    rest = jnp.concatenate(
        [
            jnp.concatenate(
                [
                    rtmp[i, b, pl.ds(0, 16, stride=2), :] + rtmp[i, b, pl.ds(1, 16, stride=2), :]
                    for b in range(5)
                ],
                axis=1,
            )
            for i in range(4)
        ],
        axis=0,
    )
    pb[...] = (total + rest * 0.25).astype(BF16)

    core = lax.div(x, 2)
    slot = lax.rem(x, 2)
    pl_copies = []
    for dx in (2, 1, 3, 0):
        for dy in (2, 1, 3, 0):
            k = dx * 4 + dy
            cpy = remote(
                pb, plin.at[slot, rows(ch, 64)], s_pl.at[k], r_pl.at[slot * 8 + ch],
                dev(s, x + dx, zh, y + dy, core),
            )
            pl_copies.append(cpy)
            if k:
                cpy.start()

    @pl.when(core != c)
    def _():
        pl_copies[-1].start()

    @pl.when(core == c)
    def _():
        plin[slot, rows(ch, 64), :] = pb[...]

    hop1(3)
    hop2(1)
    hop1(4)
    share(1, 0, 5)
    for j in range(2, 5):
        hop2(j)
    share(2, 0, 5)
    for j in range(5):
        hop3(j)
    hop4(0)
    share(3, 0, 1)

    def shared(k):
        q, j, n = shares[k]
        arrived(wall.at[pl.ds(5 * other + j, n), rows(zs[q], SLAB)], r_dd.at[k])

    for k in (0, 2, 3, 4):
        shared(k)

    pn[...] = jnp.concatenate(
        [wall[0, pl.ds(zb * SLAB + xb * 40, 40), :] for xb in range(4) for zb in range(4)], axis=0
    )
    gain, shift = g2w[:, lanes(x)], s2w[:, lanes(x)]
    inside = lax.rem(lax.broadcasted_iota(jnp.int32, (128, 1), 0), 16) < 14

    def nearest(i):
        return lax.rem(y + i + jnp.where(i == 2, 1, 0) - jnp.where(i == 3, 1, 0), 4)

    def project(i, carry):
        e, m = lax.rem(i, 2), nearest(lax.div(i, 2))
        for k in range(2):
            own = jnp.logical_and(2 * c + e == x, ch == 2 * m + k)

            @pl.when(jnp.logical_not(own))
            def _(k=k):
                arrived(plin.at[e, rows(2 * m + k, 64)], r_pl.at[e * 8 + 2 * m + k])

        p = dot(plin[e, rows(m, 128), :], pn[...]).astype(BF16)
        pjb[e, rows(m, 128), :] = p
        v = jnp.maximum(p.astype(F32) * gain + shift, 0.0)
        v = jnp.where(inside, v, 0.0)
        place = pl.ds(pl.multiple_of(128 * m + 16, 16), 128)
        abuf[0, e, place, :] = pltpu.roll(v, 1, 0).astype(BF16)
        abuf[1, e, place, :] = v.astype(BF16)
        abuf[2, e, place, :] = pltpu.roll(v, 127, 0).astype(BF16)
        return carry

    lax.fori_loop(0, 8, project, 0)

    pj_copies = []
    for e in range(2):
        for tc in range(2):
            own = jnp.logical_and(jnp.logical_and(s == 0, 2 * c + e == x), tc == c)
            src = pjb.at[e, rows(2 * y + tc, 64)]
            cpy = remote(
                src, out.at[s, :, lanes(x)], s_pj.at[2 * e + tc], r_pj.at[4 * s + x],
                dev(0, 2 * c + e, zh, y, tc),
            )
            pj_copies.append((own, cpy))

            @pl.when(jnp.logical_not(own))
            def _(cpy=cpy):
                cpy.start()

            @pl.when(own)
            def _(src=src):
                out[0, :, lanes(x)] = src[...]

    for j in range(1, 5):
        hop4(j)
    share(3, 1, 4)
    for k in (1, 5):
        shared(k)

    adds = x == y

    def c_copy(e, k):
        return remote(
            cp.at[e, rows(k, 64)], cin.at[x * 4 + y], s_c.at[e * 8 + k], r_c.at[x * 4 + y],
            dev(s, 2 * c + e, zh, lax.div(k, 2), lax.rem(k, 2)),
        )

    def c_own(e, k):
        return jnp.logical_and(2 * c + e == x, k == ch)

    def from_far(i, sign):
        step = 2 - i + jnp.where(i >= 2, 3 * (3 - i) , 0)
        step = jnp.where(i == 3, 0, step)
        return lax.rem(y + sign * step + 4, 4)

    def second(i, carry):
        e = lax.rem(lax.div(i, 4) + x, 2)
        m = from_far(lax.rem(i, 4), 1)
        a = jnp.concatenate(
            [
                abuf[t % 3, e, pl.ds(pl.multiple_of(128 * m + 16 * (t // 3), 16), 128), :]
                for t in range(9)
            ],
            axis=1,
        )
        total = dot(a, wall[pl.ds(1, 9)].reshape(9 * D, D))
        proj = pjb[e, rows(m, 128), :].astype(F32)
        cp[e, rows(m, 128), :] = (total + jnp.where(adds, proj, 0.0)).astype(BF16)
        for q in range(2):
            k = 2 * m + q
            own = c_own(e, k)

            @pl.when(jnp.logical_not(own))
            def _(k=k):
                c_copy(e, k).start()

            @pl.when(own)
            def _(k=k):
                cin[x * 4 + y] = cp[e, rows(k, 64), :]

        return carry

    lax.fori_loop(0, 8, second, 0)

    def finish(i, carry):
        yb = from_far(i, -1)
        total = jnp.zeros((64, D), F32)
        for xb in range(4):
            own = jnp.logical_and(jnp.logical_and(core == c, xb == x), yb == y)

            @pl.when(jnp.logical_not(own))
            def _(xb=xb):
                arrived(cin.at[xb * 4 + yb], r_c.at[xb * 4 + yb])

            total += cin[xb * 4 + yb].astype(F32)
        fb[:, lanes(yb)] = total.astype(BF16)

        @pl.when(s == 0)
        def _():
            f_copy(yb).start()

        @pl.when(s == 1)
        def _():
            out[1, :, lanes(yb)] = fb[:, lanes(yb)]

        return carry

    def f_copy(yb):
        block = fb.at[:, lanes(yb)]
        return remote(block, out.at[0, :, lanes(yb)], s_f.at[yb], r_f.at[yb], pair)

    lax.fori_loop(0, 4, finish, 0)

    @pl.when(s == 0)
    def _():
        for sb in range(2):
            for xb in range(4):
                own = jnp.logical_and(jnp.logical_and(sb == 0, xb == x), core == c)

                @pl.when(jnp.logical_not(own))
                def _(sb=sb, xb=xb):
                    arrived(out.at[sb, :, pl.ds(xb * D, D)], r_pj.at[4 * sb + xb])

        for yb in range(4):
            f_copy(yb).wait_send()

    @pl.when(s == 1)
    def _():
        for yb in range(4):
            arrived(out.at[0, :, pl.ds(yb * D, D)], r_f.at[yb])

    for own, cpy in pj_copies:

        @pl.when(jnp.logical_not(own))
        def _(cpy=cpy):
            cpy.wait_send()

    for e in range(2):
        for k in range(8):

            @pl.when(jnp.logical_not(c_own(e, k)))
            def _(e=e, k=k):
                c_copy(e, k).wait_send()

    px_copy.wait_send()

    @pl.when(sends_down)
    def _():
        for cpy in down:
            cpy.wait_send()

    @pl.when(sends_up)
    def _():
        for cpy in up:
            cpy.wait_send()

    @pl.when(k1_sends)
    def _():
        for cpy in k1_copies:
            cpy.wait_send()

    @pl.when(diagonal)
    def _():
        for cpy in diagonal_copies:
            cpy.wait_send()

    for goes, cpy in wy_copies + third + fourth:

        @pl.when(goes)
        def _(cpy=cpy):
            cpy.wait_send()

    @pl.when(core != c)
    def _():
        pl_copies[-1].wait_send()

    for cpy in pr_copies + kx_copies + chain + pa_copies + pl_copies[:-1]:
        cpy.wait_send()


def body(
    pixels,
    first_gain,
    first_shift,
    first_kernel,
    projection,
    second_gain,
    second_shift,
    second_kernel,
):
    dma = pltpu.SemaphoreType.DMA

    def vmem(*shape, dtype=BF16):
        return pltpu.VMEM(shape, dtype)

    counts = [
        (), (), (2,), (), (2,), (), (4, 3), (3,), (3, 3), (3, 3), (3,), (3,), (16,), (16,),
        (5,), (5,), (5,), (5,), (5,), (5,), (5,), (5,), (6,), (6,), (3,), (3,), (16,), (16,),
        (4,), (8,), (16,), (16,), (4,), (4,),
    ]
    result = pl.pallas_call(
        kernel,
        name="window",
        out_shape=jax.ShapeDtypeStruct((2, 64, 4 * D), BF16),
        in_specs=[pl.BlockSpec(memory_space=pltpu.VMEM)] * 8,
        out_specs=pl.BlockSpec(memory_space=pltpu.VMEM),
        scratch_shapes=[
            vmem(2, 8, 28, D),
            vmem(2, 1, 28, D),
            vmem(2, 1, 28, D),
            vmem(2, 112, 4 * D),
            vmem(8, 112, D),
            vmem(4, 40, D),
            vmem(10, D, D),
            vmem(D, D),
            vmem(4, 9, 40, D),
            vmem(2, 18, 32, D),
            vmem(2, 2, 19, 48, 128, dtype=F32),
            vmem(3, 2, 2, 9, 16, 256),
            vmem(256, D, dtype=F32),
            vmem(256, D),
            vmem(3, 64, D),
            vmem(4, 5, 32, 128, dtype=F32),
            vmem(64, D),
            vmem(2, 512, D),
            vmem(2, 512, D),
            vmem(3, 2, 544, D),
            vmem(2, 512, D),
            vmem(16, 64, D),
            vmem(64, 4 * D),
            vmem(1, 4 * D, dtype=F32),
            vmem(1, 4 * D, dtype=F32),
        ]
        + [dma(n) for n in counts],
        compiler_params=pltpu.CompilerParams(
            collective_id=0, has_side_effects=True, vmem_limit_bytes=56 * 2**20
        ),
        cost_estimate=pl.CostEstimate(flops=8 * 10**9, bytes_accessed=10**7, transcendentals=0),
    )(
        pixels,
        first_gain,
        first_shift,
        first_kernel.reshape(9, 40, D),
        projection,
        second_gain,
        second_shift,
        second_kernel.reshape(9, 20, 4 * D),
    )
    return result.reshape(2, 4, 16, 4 * D)[None, :, :, :14]


def solution(mesh):
    placed = (
        P("img", "ch", None, None),
        P(),
        P(),
        P(None, None, "img", None),
        P("img", None),
        P(),
        P(),
        P(None, None, ("img", "ch"), None),
    )
    return jax.shard_map(
        body,
        mesh=mesh,
        in_specs=placed,
        out_specs=P("section", "img", "ch", None, None),
        check_vma=False,
    )
```
